128 devices in a mesh: dp: 64 (over x, z, y), head: 2 (over core).
Axes of the slice: x: 4, y: 4, z: 4, core: 2. Of those that a mesh axis runs over, the one named last changes fastest.
Arguments:
- tokens: bfloat16 [98304, 512], P(('dp', 'head')), may hold values from -18 to 18
- memory: bfloat16 [98304, 512], P(('dp', 'head')), may hold values from -18 to 18
- segments: int32 [98304], P(('dp', 'head')), may hold values from 0 to 2, as said below
- mem_segments: int32 [98304], P(('dp', 'head')), may hold values from 0 to 2, as said below
- cotangent: bfloat16 [98304, 512], P(('dp', 'head')), may hold values from -6 to 6
- self_proj: bfloat16 [512, 3, 512], P(('dp', 'head')), may hold values from -0.27 to 0.27
- self_output: bfloat16 [512, 512], P(('dp', 'head')), may hold values from -0.75 to 0.75
- cross_query: bfloat16 [512, 512], P(('dp', 'head')), may hold values from -0.27 to 0.27
- cross_keyval: bfloat16 [512, 2, 512], P(('dp', 'head')), may hold values from -0.27 to 0.27
- cross_output: bfloat16 [512, 512], P(('dp', 'head')), may hold values from -0.75 to 0.75
- hidden_in: bfloat16 [512, 2048], P(('dp', 'head')), may hold values from -0.25 to 0.25
- hidden_out: bfloat16 [2048, 512], P(('dp', 'head')), may hold values from -0.1875 to 0.1875
- slot_proj: bfloat16 [1024, 512], P(('dp', 'head')), may hold values from -0.1875 to 0.1875
- norm_gain: bfloat16 [3, 512], P(None, ('dp', 'head')), may hold values from 0.5 to 1.5
- norm_bias: bfloat16 [3, 512], P(None, ('dp', 'head')), may hold values from -1.1953125 to 1.1953125
Outputs:
- out: bfloat16 [98304, 512], P(('dp', 'head'))
- grad_tokens: float32 [98304, 512], P(('dp', 'head'))
- grad_memory: float32 [98304, 512], P(('dp', 'head'))
- grad_self_proj: float32 [512, 3, 512], P(('dp', 'head'))
- grad_self_output: float32 [512, 512], P(('dp', 'head'))
- grad_cross_query: float32 [512, 512], P(('dp', 'head'))
- grad_cross_keyval: float32 [512, 2, 512], P(('dp', 'head'))
- grad_cross_output: float32 [512, 512], P(('dp', 'head'))
- grad_hidden_in: float32 [512, 2048], P(('dp', 'head'))
- grad_hidden_out: float32 [2048, 512], P(('dp', 'head'))
- grad_slot_proj: float32 [1024, 512], P(('dp', 'head'))
- grad_norm_gain: float32 [3, 512], P(None, ('dp', 'head'))
- grad_norm_bias: float32 [3, 512], P(None, ('dp', 'head'))
The draws below stay inside these ranges and needn't reach their ends.
Inputs may be any that keep to these rules, and one draw needn't show every extreme that they name: `segments`: each group of 1536 consecutive rows holds three sequences numbered 0, 1, 2 in order; sequence 1 has exactly 1152 rows and begins at one of the group's rows 1 to 383. `mem_segments`: each group of 1536 consecutive memory rows holds three sequences numbered 0, 1, 2 in order; sequence 1 has exactly 1152 rows and begins at one of the group's rows 1 to 383.
All inputs are finite; a program needn't handle non-finite values.
Results may differ from the reference program's by a relative error of at most 0.015.
Values may be sent and summed in bfloat16 or wider, within the bound.
No kernel may reach another device: no remote copies, remote signals or barrier semaphores. Data moves between devices by JAX's collectives and lax.ppermute only.
A program may use at most 192 MiB of HBM per device.

```python
import math
import jax
import jax.numpy as jnp
from jax import lax

D = 512
HEAD_DIM = 64
FF = 2048
TOK_DEV = 768
GROUP_TOK = 1536
LONG = 1152
GROUPS = 64
TOKENS = 98304


def segment_layout(key):
    starts = jax.random.randint(key, (GROUPS, 1), 1, TOK_DEV // 2)
    places = jnp.arange(GROUP_TOK, dtype=jnp.int32)[None, :]
    numbers = (places >= starts).astype(jnp.int32) + (places >= starts + LONG).astype(jnp.int32)
    return numbers.reshape(-1)


def draw_segments(key, part):
    key = jax.random.fold_in(key, 11)
    return segment_layout(key)


def draw_mem_segments(key, part):
    key = jax.random.fold_in(key, 23)
    return segment_layout(key)


def spiked(values, key):
    blocks = TOKENS // TOK_DEV
    span = D // blocks
    pairing = jax.random.permutation(key, blocks)
    row_block = jnp.arange(TOKENS, dtype=jnp.int32) // TOK_DEV
    col_block = jnp.arange(D, dtype=jnp.int32) // span
    marked = pairing[row_block][:, None] == col_block[None, :]
    return jnp.where(marked, 3.0 * values, values)


def draw_rows(key):
    value_key = jax.random.fold_in(key, 1)
    pair_key = jax.random.fold_in(key, 2)
    values = jnp.clip(jax.random.normal(value_key, (TOKENS, D), jnp.float32), -6.0, 6.0)
    return spiked(values, pair_key)


def draw_tokens(key, part):
    key = jax.random.fold_in(key, 31)
    return draw_rows(key).astype(jnp.bfloat16)


def draw_memory(key, part):
    key = jax.random.fold_in(key, 37)
    return draw_rows(key).astype(jnp.bfloat16)


def draw_matrix(key, shape):
    scale = D ** (-0.5)
    values = jnp.clip(jax.random.normal(key, shape, jnp.float32), -3.0, 3.0)
    return values * scale


def draw_self_proj(key, part):
    key = jax.random.fold_in(key, 41)
    return draw_matrix(key, (D, 3, D)).astype(jnp.bfloat16)


def draw_cross_query(key, part):
    key = jax.random.fold_in(key, 43)
    return draw_matrix(key, (D, D)).astype(jnp.bfloat16)


def draw_cross_keyval(key, part):
    key = jax.random.fold_in(key, 47)
    return draw_matrix(key, (D, 2, D)).astype(jnp.bfloat16)


def draw_norm_gain(key, part):
    key = jax.random.fold_in(key, 53)
    values = jnp.clip(0.17 * jax.random.normal(key, (3, D), jnp.float32), -0.5, 0.5)
    return (1.0 + values).astype(jnp.bfloat16)


def level_of(rng, extent, pieces, least, high):
    level, own = 1.0, jax.random.fold_in(rng, 6)
    for dim, shards_of in pieces:
        draws = jnp.exp(jax.random.uniform(jax.random.fold_in(own, dim), (shards_of,), jnp.float32, least / len(pieces), high / len(pieces)))
        level = level * jnp.repeat(draws, extent[dim] // shards_of).reshape([-1 if axis == dim else 1 for axis in range(len(extent))])
    return level


def scatter_about(own_key, shape, scale, most, shards=(), kind=jnp.bfloat16):
    loudness = level_of(own_key, shape, shards, -0.22, 0.18) if shards else 1.0
    values = jax.random.normal(own_key, shape, jnp.float32) * scale * loudness
    return jnp.minimum(jnp.maximum(values, -most), most).astype(kind)


def setup_inputs(seed: int = 0) -> dict:
    splits = jax.random.split(jax.random.key(seed), 16)
    tokens = draw_tokens(jax.random.fold_in(splits[15], 71), 0)
    memory = draw_memory(jax.random.fold_in(splits[15], 71), 0)
    segments = draw_segments(jax.random.fold_in(splits[15], 71), 0)
    mem_segments = draw_mem_segments(jax.random.fold_in(splits[15], 71), 0)
    cotangent = scatter_about(splits[4], (TOKENS, D), 1.0, 6.0, ((0, 128),))
    self_proj = draw_self_proj(jax.random.fold_in(splits[15], 71), 0)
    self_output = scatter_about(splits[6], (D, D), (D // 8) ** -0.5, 0.75, ((0, 128),))
    cross_query = draw_cross_query(jax.random.fold_in(splits[15], 71), 0)
    cross_keyval = draw_cross_keyval(jax.random.fold_in(splits[15], 71), 0)
    cross_output = scatter_about(splits[9], (D, D), (D // 8) ** -0.5, 0.75, ((0, 128),))
    hidden_in = scatter_about(splits[10], (D, FF), D ** -0.5, 0.25, ((0, 128),))
    hidden_out = scatter_about(splits[11], (FF, D), (FF // 2) ** -0.5, 0.1875, ((0, 128),))
    slot_proj = scatter_about(splits[12], (2 * D, D), (2 * D) ** -0.5, 0.1875, ((0, 128),))
    norm_gain = draw_norm_gain(jax.random.fold_in(splits[15], 71), 0)
    norm_bias = scatter_about(splits[14], (3, D), 0.3, 1.1953125, ((1, 128),))
    return dict(tokens=tokens, memory=memory, segments=segments, mem_segments=mem_segments, cotangent=cotangent, self_proj=self_proj, self_output=self_output, cross_query=cross_query, cross_keyval=cross_keyval, cross_output=cross_output, hidden_in=hidden_in, hidden_out=hidden_out, slot_proj=slot_proj, norm_gain=norm_gain, norm_bias=norm_bias)


@jax.custom_vjp
def low(v):
    return lax.optimization_barrier(v.astype(jnp.bfloat16)).astype(jnp.float32)

@jax.custom_vjp
def low_back(v):
    return v

def low_keep(v):
    return (low(v), None)

def low_pass(kept, grad):
    return (grad,)

def back_keep(v):
    return (v, None)

def back_low(kept, grad):
    return (low(grad),)
low.defvjp(low_keep, low_pass)
low_back.defvjp(back_keep, back_low)
highest = lax.Precision.HIGHEST
epsilon = 1e-05

def layer_norm(resid, gain, bias):
    center = resid - lax.optimization_barrier(jnp.mean(resid, -1, keepdims=True))
    variance = lax.optimization_barrier(jnp.mean(center * center, -1, keepdims=True))
    return center * lax.rsqrt(variance + epsilon) * gain + bias

def attention(query, keys, values, query_seg, key_seg):
    raw = jnp.einsum('qhd,khd->hqk', query, keys, precision=highest)
    scores = low_back(raw * HEAD_DIM ** (-0.5))
    allowed = query_seg[:, None] == key_seg[None, :]
    scores = jnp.where(allowed[None], scores, -1e+30)
    probs = low(jax.nn.softmax(scores, axis=-1))
    return jnp.einsum('hqk,khd->qhd', probs, values, precision=highest)

def group_layer(params, block, memory, seg, mem_seg):
    self_proj, self_output, cross_query, cross_keyval, cross_output, hidden_in, hidden_out, slot_proj, norm_gain, norm_bias = params
    rows = block.shape[0]
    mem_rows = memory.shape[0]
    heads_all = D // HEAD_DIM
    qkv = low(low_back(jnp.einsum('rd,dcf->rcf', block, self_proj, precision=highest)))
    qkv = qkv.reshape(rows, 3, heads_all, HEAD_DIM)
    mixed = attention(qkv[:, 0], qkv[:, 1], qkv[:, 2], seg, seg)
    mixed = low(low_back(mixed.reshape(rows, D)))
    resid = block + low_back(jnp.dot(mixed, self_output, precision=highest))
    first = layer_norm(resid, norm_gain[0], norm_bias[0])
    query = low(low_back(jnp.dot(low(first), cross_query, precision=highest)))
    query = query.reshape(rows, heads_all, HEAD_DIM)
    mem_kv = low(low_back(jnp.einsum('rd,dcf->rcf', memory, cross_keyval, precision=highest)))
    mem_kv = mem_kv.reshape(mem_rows, 2, heads_all, HEAD_DIM)
    crossed = attention(query, mem_kv[:, 0], mem_kv[:, 1], seg, mem_seg)
    crossed = low(low_back(crossed.reshape(rows, D)))
    resid = first + low_back(jnp.dot(crossed, cross_output, precision=highest))
    second = layer_norm(resid, norm_gain[1], norm_bias[1])
    inner = low_back(jnp.dot(low(second), hidden_in, precision=highest))
    hidden = low(jax.nn.gelu(inner))
    resid = second + low_back(jnp.dot(hidden, hidden_out, precision=highest))
    third = low(layer_norm(resid, norm_gain[2], norm_bias[2]))
    same = jnp.concatenate([seg[1:] == seg[:-1], jnp.zeros((1,), dtype=bool)])
    shifted = jnp.concatenate([third[1:], jnp.zeros((1, D), jnp.float32)])
    following = low_back(jnp.where(same[:, None], shifted, 0.0))
    paired = jnp.concatenate([third, following], -1)
    return jnp.dot(paired, slot_proj, precision=highest)

def reference(tokens, memory, segments, mem_segments, cotangent, self_proj, self_output, cross_query, cross_keyval, cross_output, hidden_in, hidden_out, slot_proj, norm_gain, norm_bias):
    params = tuple((weight.astype(jnp.float32) for weight in (self_proj, self_output, cross_query, cross_keyval, cross_output, hidden_in, hidden_out, slot_proj, norm_gain, norm_bias)))
    per_step = math.gcd(GROUPS, max(1, 4096 // GROUP_TOK))
    step_count = GROUPS // per_step

    def split(array):
        return array.reshape((step_count, per_step, GROUP_TOK) + array.shape[1:])

    def forward(weights, block, mem):

        def one_step(args):
            block_step, mem_step, seg_step, mem_seg_step = args
            return jax.vmap(lambda part_block, part_mem, part_seg, part_mem_seg: group_layer(weights, part_block, part_mem, part_seg, part_mem_seg))(block_step, mem_step, seg_step, mem_seg_step)
        result = lax.map(jax.checkpoint(one_step), (split(block), split(mem), split(segments), split(mem_segments)))
        return result.reshape(block.shape)
    primal, pullback = jax.vjp(forward, params, tokens.astype(jnp.float32), memory.astype(jnp.float32))
    grad_params, grad_tokens, grad_memory = pullback(cotangent.astype(jnp.float32))
    return (primal.astype(jnp.bfloat16), grad_tokens, grad_memory, grad_params[0], grad_params[1], grad_params[2], grad_params[3], grad_params[4], grad_params[5], grad_params[6], grad_params[7], grad_params[8], grad_params[9])
```

```python
import functools

import jax
import jax.numpy as jnp
from jax import lax
from jax.experimental import pallas as pl
from jax.experimental.pallas import tpu as pltpu
from jax.sharding import PartitionSpec as P

HEAD_DIM = 64
epsilon = 1e-05
f32 = jnp.float32
bf16 = jnp.bfloat16
ALL = ("dp", "head")
NT = (((1,), (1,)), ((), ()))
NN = (((1,), (0,)), ((), ()))
TN = (((0,), (0,)), ((), ()))
blocked = -1e30


def mm(a, b, dims=NN):
    return lax.dot_general(a, b, dims, preferred_element_type=f32)


def low_half(shape):
    return lax.broadcasted_iota(jnp.int32, shape, 1) < HEAD_DIM


def pieces(x):
    hi = x.astype(bf16)
    rest = x - hi.astype(f32)
    mid = rest.astype(bf16)
    return hi, mid, (rest - mid.astype(f32)).astype(bf16)


def fwd_kernel(size, q_ref, k_ref, v_ref, qa_ref, ka_ref, o_ref, lse_ref):
    rows = q_ref.shape[0]
    key_low = low_half(k_ref.shape)
    keys, key_extra, values = k_ref[...], ka_ref[...], v_ref[...]
    key_tiles = [jnp.where(key_low, keys, key_extra), jnp.where(key_low, key_extra, keys)]
    low = low_half((size, 128))
    for block in range(rows // size):
        here = pl.ds(block * size, size)
        q = q_ref[here, :] * bf16(HEAD_DIM**-0.5)
        qa = qa_ref[here, :]
        outs, sums = [], []
        for h in range(2):
            q_tile = jnp.where(low, q, qa) if h == 0 else jnp.where(low, qa, q)
            scores = mm(q_tile, key_tiles[h], NT)
            peak = jnp.max(scores, -1, keepdims=True)
            weights = jnp.exp(scores - peak)
            total = jnp.sum(weights, -1, keepdims=True)
            outs.append(mm(weights.astype(bf16), values) * (1.0 / total))
            sums.append(peak + jnp.log(total))
        o_ref[here, :] = jnp.where(low, outs[0], outs[1]).astype(bf16)
        lse_ref[here, :] = jnp.where(low, sums[0], sums[1])


def attend(q, kv, qa, ka, size=384):
    rows, width = q.shape
    total = kv.shape[0]
    pairs = width // 128
    row_tile = pl.BlockSpec((rows, 128), lambda p: (0, p))
    return pl.pallas_call(
        functools.partial(fwd_kernel, size),
        grid=(pairs,),
        in_specs=[
            row_tile,
            pl.BlockSpec((total, 128), lambda p: (0, p)),
            pl.BlockSpec((total, 128), lambda p: (0, p + pairs)),
            pl.BlockSpec((rows, 128), lambda p: (0, 0)),
            pl.BlockSpec((total, 128), lambda p: (0, 0)),
        ],
        out_specs=[row_tile, row_tile],
        out_shape=[jax.ShapeDtypeStruct((rows, width), bf16), jax.ShapeDtypeStruct((rows, width), f32)],
        compiler_params=pltpu.CompilerParams(vmem_limit_bytes=56 * 2**20),
        name="attend",
    )(q, kv, kv, qa, ka)


def bwd_kernel(size, q_ref, k_ref, v_ref, qa_ref, ka_ref, o_ref, lse_ref, do_ref, dq_ref, dk_ref, dv_ref, dkt, dvt):
    rows = q_ref.shape[0]
    key_low = low_half(k_ref.shape)
    keys, key_extra, values = k_ref[...], ka_ref[...], v_ref[...]
    ones = jnp.ones_like(values)
    key_tiles = [jnp.where(key_low, keys, key_extra), jnp.where(key_low, key_extra, keys)]
    value_tiles = [jnp.where(key_low, values, ones), jnp.where(key_low, ones, values)]
    low = low_half((size, 128))
    lane = lax.broadcasted_iota(jnp.int32, (size, 128), 1)
    for block in range(rows // size):
        here = pl.ds(block * size, size)
        q = q_ref[here, :] * bf16(HEAD_DIM**-0.5)
        qa = qa_ref[here, :]
        do = do_ref[here, :]
        product = do.astype(f32) * o_ref[here, :].astype(f32)
        lse = lse_ref[here, :]
        q_turned, do_turned = q.T, do.T
        dqs = []
        for h in range(2):
            spare = HEAD_DIM * (1 - h)
            mine = low if h == 0 else jnp.logical_not(low)
            delta = jnp.sum(jnp.where(mine, product, 0.0), -1, keepdims=True)
            d0, d1, d2 = pieces(-delta)
            l0, l1, l2 = pieces(-lse[:, HEAD_DIM * h : HEAD_DIM * h + 1])
            q_extra = jnp.where(lane == spare + 3, l0, jnp.where(lane == spare + 4, l1, jnp.where(lane == spare + 5, l2, qa)))
            do_extra = jnp.where(
                lane == spare, d0, jnp.where(lane == spare + 1, d1, jnp.where(lane == spare + 2, d2, bf16(0)))
            )
            probs = jnp.exp(mm(jnp.where(mine, q, q_extra), key_tiles[h], NT))
            grad = mm(jnp.where(mine, do, do_extra), value_tiles[h], NT)
            low_probs = probs.astype(bf16)
            ds = (probs * grad).astype(bf16)
            dqs.append(mm(ds, keys))
            part = slice(HEAD_DIM * h, HEAD_DIM * h + HEAD_DIM)
            new_dk = mm(q_turned[part, :], ds)
            new_dv = mm(do_turned[part, :], low_probs)
            if block == 0:
                dkt[part, :] = new_dk
                dvt[part, :] = new_dv
            else:
                dkt[part, :] += new_dk
                dvt[part, :] += new_dv
        dq_ref[here, :] = (jnp.where(low, dqs[0], dqs[1]) * HEAD_DIM**-0.5).astype(bf16)
    dk_ref[...] = dkt[...].astype(bf16).T
    dv_ref[...] = dvt[...].astype(bf16).T


def attend_back(q, kv, qa, ka, o, lse, do, size=384):
    rows, width = q.shape
    total = kv.shape[0]
    pairs = width // 128
    row_tile = pl.BlockSpec((rows, 128), lambda p: (0, p))
    key_tile = pl.BlockSpec((total, 128), lambda p: (0, p))
    return pl.pallas_call(
        functools.partial(bwd_kernel, size),
        grid=(pairs,),
        in_specs=[
            row_tile,
            key_tile,
            pl.BlockSpec((total, 128), lambda p: (0, p + pairs)),
            pl.BlockSpec((rows, 128), lambda p: (0, 0)),
            pl.BlockSpec((total, 128), lambda p: (0, 0)),
            row_tile,
            row_tile,
            row_tile,
        ],
        out_specs=[row_tile, key_tile, key_tile],
        out_shape=[
            jax.ShapeDtypeStruct((rows, width), bf16),
            jax.ShapeDtypeStruct((total, width), bf16),
            jax.ShapeDtypeStruct((total, width), bf16),
        ],
        scratch_shapes=[pltpu.VMEM((128, total), f32), pltpu.VMEM((128, total), f32)],
        compiler_params=pltpu.CompilerParams(vmem_limit_bytes=56 * 2**20),
        name="attend_back",
    )(q, kv, kv, qa, ka, o, lse, do)


def extras(query_seg, key_seg):
    lane = jnp.arange(128) % HEAD_DIM
    marks = lane[None] < 3
    qa = jnp.where(marks & (query_seg[:, None] != lane[None]), blocked, 0.0).astype(bf16)
    ones = (lane[None] >= 3) & (lane[None] < 6)
    ka = ((marks & (key_seg[:, None] == lane[None])) | ones).astype(bf16)
    return qa, ka


def norm_forward(resid, gain, bias):
    center = resid - jnp.mean(resid, -1, keepdims=True)
    inverse = lax.rsqrt(jnp.mean(center * center, -1, keepdims=True) + epsilon)
    normed = center * inverse
    return (normed * gain + bias, normed, inverse)


def norm_backward(upstream, normed, inverse, gain):
    scaled = upstream * gain
    grad_in = inverse * (
        scaled - jnp.mean(scaled, -1, keepdims=True) - normed * jnp.mean(scaled * normed, -1, keepdims=True)
    )
    return (grad_in, jnp.sum(upstream * normed, 0), jnp.sum(upstream, 0))


def swap(value):
    return lax.ppermute(value, "head", [(0, 1), (1, 0)])


def tie(*values):
    return lax.optimization_barrier(values)


def by_core(own, other, axis):
    first = lax.axis_index("head") == 0
    return jnp.where(first, jnp.concatenate([own, other], axis), jnp.concatenate([other, own], axis))


def half(value, core):
    width = value.shape[-1] // 2
    return lax.dynamic_slice_in_dim(value, core * width, width, value.ndim - 1)


EARLY = 2176
LATE = 2560
LIMIT = pltpu.CompilerParams(vmem_limit_bytes=40 * 2**20)


def whole(count):
    return [pl.BlockSpec(memory_space=pltpu.VMEM)] * count


def shape(rows, columns, kind=bf16):
    return jax.ShapeDtypeStruct((rows, columns), kind)


def project_kernel(head, own, other, tok, tok2, mem, mem2, q, kv, mkv, w_self, w_out, w_query, w_kv, w_cross, norms):
    first = head[0, 0] == 0

    def both(slot):
        here = slice(256 * slot, 256 * slot + 256)
        a, b = own[:, here], other[:, here]
        return jnp.concatenate([jnp.where(first, a, b), jnp.where(first, b, a)], 1)

    for part in range(3):
        w_self[:, 512 * part : 512 * part + 512] = both(part)
    rows = tok.shape[0]
    q[...] = mm(tok[...], w_self[:, :512]).astype(bf16)
    kv[:rows, :] = mm(tok[...], w_self[:, 512:]).astype(bf16)
    kv[rows:, :] = mm(tok2[...], w_self[:, 512:]).astype(bf16)
    w_out[...] = both(3)
    w_query[...] = both(4)
    w_kv[:, :512] = both(5)
    w_kv[:, 512:] = both(6)
    w_cross[...] = both(7)
    mkv[:rows, :] = mm(mem[...], w_kv[...]).astype(bf16)
    mkv[rows:, :] = mm(mem2[...], w_kv[...]).astype(bf16)
    norms[...] = own[:, 2048:].astype(f32).T[:8, :]


def project(head, own, other, tok, tok2, mem, mem2):
    rows = tok.shape[0]
    return pl.pallas_call(
        project_kernel,
        in_specs=[pl.BlockSpec(memory_space=pltpu.SMEM)] + whole(6),
        out_specs=whole(9),
        out_shape=[
            shape(rows, 512),
            shape(2 * rows, 1024),
            shape(2 * rows, 1024),
            shape(512, 1536),
            shape(512, 512),
            shape(512, 512),
            shape(512, 1024),
            shape(512, 512),
            shape(8, 512, f32),
        ],
        compiler_params=LIMIT,
        name="project",
    )(head, own, other, tok, tok2, mem, mem2)


def one_hot(rows, columns, target):
    row = lax.broadcasted_iota(jnp.int32, (rows, columns), 0)
    column = lax.broadcasted_iota(jnp.int32, (rows, columns), 1)
    return jnp.where(target(row) == column, 1.0, 0.0).astype(bf16)


def spread_units(row):
    return ((row >> 3) & 3) * 128 + (row >> 5) * 8 + (row & 7)


def spread_rows(row):
    return ((row >> 3) & 1) * 256 + (row >> 4) * 8 + (row & 7)


def norm(resid, gain, bias):
    center = resid - jnp.mean(resid, -1, keepdims=True)
    inverse = lax.rsqrt(jnp.mean(center * center, -1, keepdims=True) + epsilon)
    normed = center * inverse
    return normed * gain + bias, normed, inverse


def norm_back(upstream, normed, inverse, gain):
    scaled = upstream * gain
    mean = jnp.mean(scaled, -1, keepdims=True)
    slope = jnp.mean(scaled * normed, -1, keepdims=True)
    return inverse * (scaled - mean - normed * slope)


def gelu(v):
    root = 0.7978845608028654
    square = v * v
    t = jnp.tanh(root * (v + 0.044715 * square * v))
    up = 0.5 * (1.0 + t)
    return v * up, up + 0.5 * v * (1.0 - t * t) * (root * (1.0 + 3 * 0.044715 * square))


def forward_back_kernel(
    size, head, own, other, mix, first, w_cross, norms, cot, cot_behind,
    third_out, slot, keep, send, resid_grad, mix_grad, norm_grads,
    w_in, w_out, hidden, inner_grad, second, branch_three, branch_two, third_spread,
):
    rows = mix.shape[0]
    core = head[0, 0]

    def packed(side, here, lanes):
        return jnp.where(core == side, own[here, lanes], other[here, lanes])

    units = one_hot(512, 512, spread_units)
    every = slice(0, 512)
    for chunk in range(4):
        start = 512 * (chunk % 2)
        moved = mm(packed(chunk // 2, every, slice(start, start + 512)), units).astype(bf16)
        for k in range(4):
            w_in[:, 512 * k + 128 * chunk : 512 * k + 128 * chunk + 128] = moved[:, 128 * k : 128 * k + 128]
    for k in range(4):
        for side in range(2):
            w_out[512 * k : 512 * k + 512, 256 * side : 256 * side + 256] = packed(
                side, every, slice(1024 + 256 * k, 1280 + 256 * k)
            )
    order = one_hot(512, 512, spread_rows)
    for side in range(2):
        for level in range(2):
            here = slice(256 * level, 256 * level + 256)
            stack = jnp.concatenate([packed(side, here, slice(2048 + 256 * k, 2304 + 256 * k)) for k in range(2)], 0)
            slot[512 * level : 512 * level + 512, 256 * side : 256 * side + 256] = mm(order, stack).astype(bf16)
    gain_two, gain_three = norms[1:2, :], norms[2:3, :]
    bias_two, bias_three = norms[4:5, :], norms[5:6, :]
    sums = [jnp.zeros((1, 512), f32) for _ in range(4)]
    for block in range(rows // size):
        here = pl.ds(block * size, size)
        resid = first[here, :] + mm(mix[here, :], w_cross[...])
        second_block, normed_two, inverse_two = norm(resid, gain_two, bias_two)
        second_low = second_block.astype(bf16)
        second[here, :] = second_low
        resid = second_block
        slopes = []
        for k in range(4):
            part = slice(512 * k, 512 * k + 512)
            value, slope = gelu(mm(second_low, w_in[:, part]))
            value = value.astype(bf16)
            hidden[here, part] = value
            slopes.append(slope)
            resid = resid + mm(value, w_out[part, :])
        third, normed_three, inverse_three = norm(resid, gain_three, bias_three)
        third_low = third.astype(bf16)
        third_out[here, :] = third_low
        third_spread[here, :] = mm(third_low, order, NN).astype(bf16)
        grad = mm(cot[here, :], slot[:512, :], NT) + mm(cot_behind[here, :], slot[512:, :], NT)
        sums[1] += jnp.sum(grad * normed_three, 0, keepdims=True)
        sums[3] += jnp.sum(grad, 0, keepdims=True)
        grad = norm_back(grad, normed_three, inverse_three, gain_three)
        branch = grad.astype(bf16)
        branch_three[here, :] = branch
        for k in range(4):
            part = slice(512 * k, 512 * k + 512)
            inner = (mm(branch, w_out[part, :], NT) * slopes[k]).astype(bf16)
            inner_grad[here, part] = inner
            grad = grad + mm(inner, w_in[:, part], NT)
        sums[0] += jnp.sum(grad * normed_two, 0, keepdims=True)
        sums[2] += jnp.sum(grad, 0, keepdims=True)
        grad = norm_back(grad, normed_two, inverse_two, gain_two)
        resid_grad[here, :] = grad
        branch = grad.astype(bf16)
        branch_two[here, :] = branch
        mix_grad[here, :] = mm(branch, w_cross[...], NT).astype(bf16)
    norm_grads[...] = jnp.concatenate(sums + [jnp.zeros((4, 512), f32)], 0)

    targets = ((keep, core), (send, 1 - core))
    third_turned = third_spread[...].T
    mix_turned = mix[...].T
    second_turned = second[...].T
    for target, side in targets:
        columns = pl.ds(pl.multiple_of(side * 256, 256), 256)
        near, behind = cot[:, columns], cot_behind[:, columns]
        for k in range(2):
            lanes = slice(2048 + 256 * k, 2304 + 256 * k)
            target[:256, lanes] = mm(third_turned[256 * k : 256 * k + 256, :], near).astype(bf16)
            target[256:, lanes] = mm(third_turned[256 * k : 256 * k + 256, :], behind).astype(bf16)
        target[:, LATE : LATE + 256] = mm(mix_turned, branch_two[:, columns]).astype(bf16)
    for k in range(4):
        turned = hidden[:, 512 * k : 512 * k + 512].T
        for target, side in targets:
            columns = pl.ds(pl.multiple_of(side * 256, 256), 256)
            target[:, 1024 + 256 * k : 1280 + 256 * k] = mm(turned, branch_three[:, columns]).astype(bf16)
    for target, side in targets:
        for chunk in range(2):
            pieces_here = []
            for k in range(4):
                start = pl.multiple_of(512 * k + 256 * side + 128 * chunk, 128)
                pieces_here.append(inner_grad[:, pl.ds(start, 128)])
            grad = mm(second_turned, jnp.concatenate(pieces_here, 1)).astype(bf16)
            target[:, 512 * chunk : 512 * chunk + 512] = mm(grad, units, NT).astype(bf16)


def forward_back(head, own, other, mix, first, w_cross, norms, cot, cot_behind, size=256):
    rows = mix.shape[0]
    return pl.pallas_call(
        functools.partial(forward_back_kernel, size),
        in_specs=[pl.BlockSpec(memory_space=pltpu.SMEM)] + whole(8),
        out_specs=whole(7),
        out_shape=[
            shape(rows, 512),
            shape(1024, 512),
            shape(512, LATE + 256),
            shape(512, LATE + 256),
            shape(rows, 512, f32),
            shape(rows, 512),
            shape(8, 512, f32),
        ],
        scratch_shapes=[
            pltpu.VMEM((512, 2048), bf16),
            pltpu.VMEM((2048, 512), bf16),
            pltpu.VMEM((rows, 2048), bf16),
            pltpu.VMEM((rows, 2048), bf16),
            pltpu.VMEM((rows, 512), bf16),
            pltpu.VMEM((rows, 512), bf16),
            pltpu.VMEM((rows, 512), bf16),
            pltpu.VMEM((rows, 512), bf16),
        ],
        compiler_params=LIMIT,
        name="forward_back",
    )(head, own, other, mix, first, w_cross, norms, cot, cot_behind)


LAST = 1920


def grads_kernel(
    head, tok, tok2, mem, mem2, first_low, mix, branch, q_self, k_self, v_self, q_cross, k_cross, v_cross, norm_grads,
    keep, send,
):
    core = head[0, 0]
    rows = tok.shape[0]
    tok_t, tok2_t, mem_t, mem2_t = tok[...].T, tok2[...].T, mem[...].T, mem2[...].T
    first_t, mix_t = first_low[...].T, mix[...].T
    for target, side in ((keep, core), (send, 1 - core)):
        columns = pl.ds(pl.multiple_of(side * 256, 256), 256)

        def put(slot, value):
            target[:, 256 * slot : 256 * slot + 256] = value.astype(bf16)

        def pair(a, b, grad):
            return mm(a, grad[:rows, columns]) + mm(b, grad[rows:, columns])

        put(0, mm(tok_t, q_self[:, columns]))
        put(1, pair(tok_t, tok2_t, k_self))
        put(2, pair(tok_t, tok2_t, v_self))
        put(3, mm(mix_t, branch[:, columns]))
        put(4, mm(first_t, q_cross[:, columns]))
        put(5, pair(mem_t, mem2_t, k_cross))
        put(6, pair(mem_t, mem2_t, v_cross))
        padded = jnp.concatenate([norm_grads[...], jnp.zeros((120, 512), f32)], 0)
        target[:, 1792:] = padded.T.astype(bf16)


def grads(head, *values):
    return pl.pallas_call(
        grads_kernel,
        in_specs=[pl.BlockSpec(memory_space=pltpu.SMEM)] + whole(14),
        out_specs=whole(2),
        out_shape=[shape(512, LAST), shape(512, LAST)],
        compiler_params=LIMIT,
        name="grads",
    )(head, *values)


def to_owners(keep, arrived):
    mine = (keep.astype(f32) + arrived.astype(f32)).astype(bf16).reshape(64, 8, keep.shape[1])
    return lax.all_to_all(mine, "dp", split_axis=0, concat_axis=0, tiled=True)


def owned(sums):
    core = lax.axis_index("head")
    mine = lax.dynamic_slice_in_dim(sums, core * 4, 4, 0)
    other = swap(lax.dynamic_slice_in_dim(sums, 4 - core * 4, 4, 0))
    return mine, other


def joined(mine, other, *slots):
    return jnp.concatenate([by_core(mine[:, s : s + 256], other[:, s : s + 256], 1) for s in slots], 1)


def shards(
    tokens,
    memory,
    segments,
    mem_segments,
    cotangent,
    self_proj,
    self_output,
    cross_query,
    cross_keyval,
    cross_output,
    hidden_in,
    hidden_out,
    slot_proj,
    norm_gain,
    norm_bias,
):
    rows = tokens.shape[0]
    core = lax.axis_index("head")
    head = core.astype(jnp.int32).reshape(1, 1)

    norms = jnp.concatenate([norm_gain, norm_bias, jnp.zeros((122, 4), bf16)]).T
    weights = [self_proj[:, 0], self_proj[:, 1], self_proj[:, 2], self_output, cross_query]
    weights += [cross_keyval[:, 0], cross_keyval[:, 1], cross_output]
    early = [jnp.concatenate([half(w, c) for w in weights] + [norms], 1) for c in (core, 1 - core)]
    early = by_core(early[0], swap(early[1]), 0)
    late = [half(w, c) for c in (core, 1 - core) for w in (hidden_in, hidden_out, slot_proj)]
    late_sent = jnp.concatenate([late[3][:, :512], late[3][:, 512:]], 0)
    late_sent = swap(jnp.concatenate([late_sent, late[4][:8], late[4][8:], late[5]], 1))
    late_in = jnp.concatenate([late_sent[:4, :512], late_sent[4:, :512]], 1)
    late = jnp.concatenate(
        [
            by_core(late[0], late_in, 0),
            by_core(jnp.concatenate([late[1][:8], late[1][8:]], 1), late_sent[:, 512:1024], 1),
            by_core(late[2], late_sent[:, 1024:], 1),
        ],
        1,
    )
    late = lax.all_gather(late, "dp", axis=0, tiled=True)

    early = jnp.broadcast_to(early[None], (64, 8, EARLY))
    early = lax.all_to_all(early, "dp", split_axis=0, concat_axis=0, tiled=True).reshape(512, EARLY)
    early_other = swap(early)

    other_tokens, other_memory = swap(tokens), swap(memory)
    other_seg, other_mem_seg = swap(segments), swap(mem_segments)
    other_cot = swap(cotangent[-1:])
    self_qa, self_ka = extras(segments, jnp.concatenate([segments, other_seg]))
    cross_qa, cross_ka = extras(segments, jnp.concatenate([mem_segments, other_mem_seg]))
    before = jnp.concatenate([jnp.where(core == 1, other_seg[-1:], -1), segments[:-1]])
    after = jnp.concatenate([segments[1:], jnp.where(core == 0, other_seg[:1], -1)])
    cot_behind = jnp.where((before == segments)[:, None], jnp.concatenate([other_cot, cotangent[:-1]]), bf16(0))
    same_after = (after == segments)[:, None]

    query, keyval, mem_keyval, w_self, w_out, w_query, w_kv, w_cross, norms = project(
        head, early, early_other, tokens, other_tokens, memory, other_memory
    )
    self_mix, self_lse = attend(query, keyval, self_qa, self_ka)
    resid = tokens.astype(f32) + mm(self_mix, w_out)
    first, first_normed, first_inv = norm_forward(resid, norms[0], norms[3])
    first_low = first.astype(bf16)
    cross_q = mm(first_low, w_query).astype(bf16)
    cross_mix, cross_lse = attend(cross_q, mem_keyval, cross_qa, cross_ka)
    late, cross_mix = tie(late, cross_mix)
    third_low, slot, keep, send, grad_resid, grad_cross_mix, norm_grads = forward_back(
        head, late, swap(late), cross_mix, first, w_cross, norms, cotangent, cot_behind
    )
    other_third = swap(third_low[:1])
    keep, arrived, grad_cross_mix = tie(keep, swap(send), grad_cross_mix)
    late_sums = to_owners(keep, arrived)

    dq_cross, dk_cross, dv_cross = attend_back(
        cross_q, mem_keyval, cross_qa, cross_ka, cross_mix, cross_lse, grad_cross_mix
    )
    other_dk, other_dv = swap(dk_cross[rows:]), swap(dv_cross[rows:])
    grad_first = grad_resid + mm(dq_cross, w_query, NT)
    grad_resid, gain_one, bias_one = norm_backward(grad_first, first_normed, first_inv, norms[0])
    branch = grad_resid.astype(bf16)
    grad_self_mix = mm(branch, w_out, NT).astype(bf16)
    dq, dk, dv = attend_back(query, keyval, self_qa, self_ka, self_mix, self_lse, grad_self_mix)
    dq, dk, dv, late_sums = tie(dq, dk, dv, late_sums)
    norm_grads = jnp.concatenate([gain_one[None], norm_grads[:2], bias_one[None], norm_grads[2:6]])
    keep, send = grads(
        head, tokens, other_tokens, memory, other_memory, first_low, self_mix, branch,
        dq, dk, dv, dq_cross, dk_cross, dv_cross, norm_grads,
    )
    last_sums = to_owners(keep, swap(send))

    sums = jnp.sum(late_sums.astype(f32), 0)
    mine, other = owned(jnp.concatenate([sums[:, :1024], sums[:, LATE:]], 1))
    tall = [
        jnp.concatenate([half(sums[:, 1024:2048], c), half(sums[:, 2048:LATE], c)], 1) for c in (core, 1 - core)
    ]
    tall, tall_other = tall[0], swap(tall[1])
    dmk = (dk_cross[:rows].astype(f32) + other_dk.astype(f32)).astype(bf16)
    dmv = (dv_cross[:rows].astype(f32) + other_dv.astype(f32)).astype(bf16)
    other_dk, other_dv = swap(dk[rows:]), swap(dv[rows:])
    following = jnp.where(same_after, jnp.concatenate([third_low[1:], other_third]), bf16(0))
    out = (mm(third_low, slot[:512]) + mm(following, slot[512:])).astype(bf16)
    grad_memory = mm(dmk, w_kv[:, :512], NT) + mm(dmv, w_kv[:, 512:], NT)
    dsk = (dk[:rows].astype(f32) + other_dk.astype(f32)).astype(bf16)
    dsv = (dv[:rows].astype(f32) + other_dv.astype(f32)).astype(bf16)
    grad_tokens = grad_resid + mm(dq, w_self[:, :512], NT)
    grad_tokens = grad_tokens + mm(dsk, w_self[:, 512:1024], NT) + mm(dsv, w_self[:, 1024:], NT)
    g_hidden_in = by_core(mine[:, :1024], other[:, :1024], 1)
    g_hidden_out = jnp.concatenate([joined(tall, tall_other, 0), joined(tall, tall_other, 256)])
    g_slot = joined(tall, tall_other, 512)
    out, grad_memory, grad_tokens, last_sums = tie(out, grad_memory, grad_tokens, last_sums)
    last, last_other = owned(jnp.sum(last_sums.astype(f32), 0))
    g_norm = last[:, 1792:1798].T
    return (
        out,
        grad_tokens,
        grad_memory,
        joined(last, last_other, 0, 256, 512).reshape(4, 3, 512),
        joined(last, last_other, 768),
        joined(last, last_other, 1024),
        joined(last, last_other, 1280, 1536).reshape(4, 2, 512),
        joined(mine, other, 1024),
        g_hidden_in,
        g_hidden_out,
        g_slot,
        g_norm[:3],
        g_norm[3:],
    )


def solution(mesh):
    split = P(ALL, None)
    cube = P(ALL, None, None)
    flat = P(ALL)
    columns = P(None, ALL)
    in_specs = (split, split, flat, flat, split, cube, split, split, cube, split, split, split, split, columns, columns)
    out_specs = (split, split, split, cube, split, split, cube, split, split, split, split, columns, columns)
    return jax.shard_map(shards, mesh=mesh, in_specs=in_specs, out_specs=out_specs, check_vma=False)
```

```python
import functools

import jax
import jax.numpy as jnp
from jax import lax
from jax.experimental import pallas as pl
from jax.experimental.pallas import tpu as pltpu
from jax.sharding import PartitionSpec as P

HEAD_DIM = 64
epsilon = 1e-05
f32 = jnp.float32
bf16 = jnp.bfloat16
ALL = ("dp", "head")
NT = (((1,), (1,)), ((), ()))
NN = (((1,), (0,)), ((), ()))
TN = (((0,), (0,)), ((), ()))
blocked = -1e30


def mm(a, b, dims=NN):
    return lax.dot_general(a, b, dims, preferred_element_type=f32)


def low_half(shape):
    return lax.broadcasted_iota(jnp.int32, shape, 1) < HEAD_DIM


def pieces(x):
    hi = x.astype(bf16)
    rest = x - hi.astype(f32)
    mid = rest.astype(bf16)
    return hi, mid, (rest - mid.astype(f32)).astype(bf16)


def attention(q_ref, kv_ref, qa_ref, ka_ref, o_ref, lse_ref, size=768):
    rows, width = q_ref.shape
    total = kv_ref.shape[0]

    def pair(p, carry):
        here = pl.ds(pl.multiple_of(128 * p, 128), 128)
        key_low = low_half((total, 128))
        keys, key_extra = kv_ref[:, here], ka_ref[...]
        key_tiles = [jnp.where(key_low, keys, key_extra), jnp.where(key_low, key_extra, keys)]
        turned = kv_ref[:, pl.ds(pl.multiple_of(128 * p + width, 128), 128)].T
        ones = jnp.ones((16, total), bf16)
        value_tiles = [jnp.concatenate([turned[64 * h : 64 * h + 64], ones], 0) for h in range(2)]
        low = low_half((size, 128))
        for block in range(rows // size):
            span = slice(block * size, block * size + size)
            q = q_ref[span, here] * bf16(HEAD_DIM**-0.5)
            qa = qa_ref[span, :]
            outs, sums = [], []
            for h in range(2):
                q_tile = jnp.where(low, q, qa) if h == 0 else jnp.where(low, qa, q)
                scores = mm(key_tiles[h], q_tile, NT)
                peak = jnp.max(scores, 0, keepdims=True)
                mixed = mm(value_tiles[h], jnp.exp(scores - peak).astype(bf16))
                count = mixed[64:65, :]
                outs.append(mixed[:64, :] * (1.0 / count))
                sums.append(peak + jnp.log(count))
            o_ref[span, here] = jnp.concatenate(outs, 0).T.astype(bf16)
            lse_ref[p, :, span] = jnp.concatenate(sums + [jnp.zeros((6, size), f32)], 0)
        return carry

    lax.fori_loop(0, width // 128, pair, 0)


def attention_back(
    q_ref, kv_ref, qa_ref, ka_ref, o_ref, lse_ref, do_ref, dq_ref, dk_ref, dk2_ref, dv_ref, dv2_ref, dkt, dvt, size=384
):
    rows, width = q_ref.shape
    total = kv_ref.shape[0]

    def pair(p, carry):
        lanes = pl.ds(pl.multiple_of(128 * p, 128), 128)
        key_low = low_half((total, 128))
        keys, key_extra = kv_ref[:, lanes], ka_ref[...]
        values = kv_ref[:, pl.ds(pl.multiple_of(128 * p + width, 128), 128)]
        ones = jnp.ones_like(values)
        key_tiles = [jnp.where(key_low, keys, key_extra), jnp.where(key_low, key_extra, keys)]
        value_tiles = [jnp.where(key_low, values, ones), jnp.where(key_low, ones, values)]
        low = low_half((size, 128))
        lane = lax.broadcasted_iota(jnp.int32, (size, 128), 1)
        lse_columns = lse_ref[p].T
        for block in range(rows // size):
            here = slice(block * size, block * size + size)
            q = q_ref[here, lanes] * bf16(HEAD_DIM**-0.5)
            qa = qa_ref[here, :]
            do = do_ref[here, lanes]
            product = do.astype(f32) * o_ref[here, lanes].astype(f32)
            lse = lse_columns[here, :]
            q_turned, do_turned = q.T, do.T
            dqs = []
            for h in range(2):
                spare = HEAD_DIM * (1 - h)
                mine = low if h == 0 else jnp.logical_not(low)
                delta = jnp.sum(jnp.where(mine, product, 0.0), -1, keepdims=True)
                d0, d1, d2 = pieces(-delta)
                l0, l1, l2 = pieces(-lse[:, h : h + 1])
                q_extra = jnp.where(
                    lane == spare + 3, l0, jnp.where(lane == spare + 4, l1, jnp.where(lane == spare + 5, l2, qa))
                )
                do_extra = jnp.where(
                    lane == spare, d0, jnp.where(lane == spare + 1, d1, jnp.where(lane == spare + 2, d2, bf16(0)))
                )
                probs = jnp.exp(mm(jnp.where(mine, q, q_extra), key_tiles[h], NT))
                grad = mm(jnp.where(mine, do, do_extra), value_tiles[h], NT)
                low_probs = probs.astype(bf16)
                ds = (probs * grad).astype(bf16)
                dqs.append(mm(ds, keys))
                part = slice(HEAD_DIM * h, HEAD_DIM * h + HEAD_DIM)
                new_dk = mm(q_turned[part, :], ds)
                new_dv = mm(do_turned[part, :], low_probs)
                if block == 0:
                    dkt[part, :] = new_dk
                    dvt[part, :] = new_dv
                else:
                    dkt[part, :] += new_dk
                    dvt[part, :] += new_dv
            dq_ref[here, lanes] = (jnp.where(low, dqs[0], dqs[1]) * HEAD_DIM**-0.5).astype(bf16)
        for turned, near, far in ((dkt, dk_ref, dk2_ref), (dvt, dv_ref, dv2_ref)):
            near[:, lanes] = turned[:, :rows].astype(bf16).T
            far[:, lanes] = turned[:, rows:].astype(bf16).T
        return carry

    lax.fori_loop(0, width // 128, pair, 0)


def extras(query_seg, key_seg):
    lane = jnp.arange(128) % HEAD_DIM
    marks = lane[None] < 3
    qa = jnp.where(marks & (query_seg[:, None] != lane[None]), blocked, 0.0).astype(bf16)
    ones = (lane[None] >= 3) & (lane[None] < 6)
    ka = ((marks & (key_seg[:, None] == lane[None])) | ones).astype(bf16)
    return qa, ka


def swap(value):
    return lax.ppermute(value, "head", [(0, 1), (1, 0)])


def tie(*values):
    return lax.optimization_barrier(values)


def by_core(own, other, axis):
    first = lax.axis_index("head") == 0
    return jnp.where(first, jnp.concatenate([own, other], axis), jnp.concatenate([other, own], axis))


def half(value, core):
    width = value.shape[-1] // 2
    return lax.dynamic_slice_in_dim(value, core * width, width, value.ndim - 1)


def halves(*weights):
    sides = [jnp.concatenate([w[:, w.shape[1] // 2 * i : w.shape[1] // 2 * (i + 1)] for w in weights], 1) for i in (0, 1)]
    first = lax.axis_index("head") == 0
    return jnp.where(first, sides[0], sides[1]), jnp.where(first, sides[1], sides[0])


EARLY = 1152
MIDDLE = 768
LATE = 2816
CROSS, OUT, SLOT = 1024, 1280, 2304


def staged(body, name, head, values, outs, scratch=(), limit=60):
    count, results = len(values), len(outs)
    spans = [v[1:] if isinstance(v, tuple) else None for v in values]
    values = [v[0] if isinstance(v, tuple) else v for v in values]
    sizes = [v.shape if span is None else (v.shape[0], span[1] - span[0]) for v, span in zip(values, spans)]

    def kernel(*refs):
        head_ref, sources, targets = refs[0], refs[1 : 1 + count], refs[1 + count : 1 + count + results]
        rest = refs[1 + count + results :]
        inside, made = rest[:count], rest[count : count + results]
        in_sems, out_sems = rest[count + results], rest[count + results + 1]
        loads = []
        for i in range(count):
            source = sources[i] if spans[i] is None else sources[i].at[:, spans[i][0] : spans[i][1]]
            loads.append(pltpu.make_async_copy(source, inside[i], in_sems.at[i]))
            loads[i].start()
        waited, stores = set(), []

        def get(i):
            if i not in waited:
                loads[i].wait()
                waited.add(i)
            return inside[i]

        def put(i):
            store = pltpu.make_async_copy(made[i], targets[i], out_sems.at[i])
            store.start()
            stores.append(store)

        body(head_ref[0, 0], get, made, put, *rest[count + results + 2 :])
        for i in range(count):
            get(i)
        for store in stores:
            store.wait()

    return pl.pallas_call(
        kernel,
        in_specs=[pl.BlockSpec(memory_space=pltpu.SMEM)] + [pl.BlockSpec(memory_space=pltpu.HBM)] * count,
        out_specs=[pl.BlockSpec(memory_space=pltpu.HBM)] * results,
        out_shape=outs,
        scratch_shapes=[pltpu.VMEM(size, v.dtype) for size, v in zip(sizes, values)]
        + [pltpu.VMEM(o.shape, o.dtype) for o in outs]
        + [pltpu.SemaphoreType.DMA((count,)), pltpu.SemaphoreType.DMA((results,))]
        + list(scratch),
        compiler_params=pltpu.CompilerParams(vmem_limit_bytes=limit * 2**20),
        name=name,
    )(head, *values)


def in_fours(rows):
    place = lax.broadcasted_iota(jnp.int32, (1, 512), 1) & 3
    moved = {s: pltpu.roll(rows, s % 512, 1) for s in range(-3, 4)}
    made = []
    for base in (0, 4):
        for c in range(4):
            row = jnp.zeros((1, 512), f32)
            for n in range(4):
                row = row + jnp.where(place == n, moved[n - c][base + n : base + n + 1, :], 0.0)
            made.append(row)
    return jnp.concatenate(made, 0)


def shape(rows, columns, kind=bf16):
    return jax.ShapeDtypeStruct((rows, columns), kind)


def both_halves(core, own, other, slot):
    here = slice(256 * slot, 256 * slot + 256)
    a, b = own[:, here], other[:, here]
    return jnp.concatenate([jnp.where(core == 0, a, b), jnp.where(core == 0, b, a)], 1)


def forward_self(head, own, other, tok, tok2, qa, ka):
    rows = tok.shape[0]

    def body(core, get, made, put):
        q, kv, w_self, w_out, norms, mix, lse, first, low = made
        own, other = get(0), get(1)
        for part in range(3):
            w_self[:, 512 * part : 512 * part + 512] = both_halves(core, own, other, part)
        put(2)
        q[...] = mm(get(2)[...], w_self[:, :512]).astype(bf16)
        put(0)
        kv[:rows, :] = mm(get(2)[...], w_self[:, 512:]).astype(bf16)
        kv[rows:, :] = mm(get(3)[...], w_self[:, 512:]).astype(bf16)
        put(1)
        w_out[...] = both_halves(core, own, other, 3)
        put(3)
        turned = in_fours(own[:, 1024:].astype(f32).T[:8, :])
        norms[...] = jnp.concatenate([turned[:3, :], turned[4:7, :], jnp.zeros((2, 512), f32)], 0)
        put(4)
        attention(q, kv, get(4), get(5), mix, lse)
        put(5)
        put(6)
        size = rows // 2
        for block in range(2):
            here = slice(block * size, block * size + size)
            value = get(2)[here, :].astype(f32) + mm(mix[here, :], w_out[...])
            value = norm(value, norms[0:1, :], norms[3:4, :])[0]
            first[here, :] = value
            low[here, :] = value.astype(bf16)
        put(8)
        put(7)

    outs = [shape(rows, 512), shape(2 * rows, 1024), shape(512, 1536), shape(512, 512), shape(8, 512, f32)]
    outs += [shape(rows, 512), jax.ShapeDtypeStruct((4, 8, rows), f32), shape(rows, 512, f32), shape(rows, 512)]
    return staged(body, "forward_self", head, [(own, 0, EARLY), (other, 0, EARLY), tok, tok2, qa, ka], outs)


def forward_cross(head, own, other, low, mem, mem2, qa, ka):
    rows = mem.shape[0]

    def body(core, get, made, put):
        q, kv, w_query, w_kv, mix, lse = made
        own, other = get(0), get(1)
        w_query[...] = both_halves(core, own, other, 0)
        w_kv[:, :512] = both_halves(core, own, other, 1)
        w_kv[:, 512:] = both_halves(core, own, other, 2)
        put(2)
        put(3)
        q[...] = mm(get(2)[...], w_query[...]).astype(bf16)
        put(0)
        kv[:rows, :] = mm(get(3)[...], w_kv[...]).astype(bf16)
        kv[rows:, :] = mm(get(4)[...], w_kv[...]).astype(bf16)
        put(1)
        attention(q, kv, get(5), get(6), mix, lse)
        put(4)
        put(5)

    outs = [shape(rows, 512), shape(2 * rows, 1024), shape(512, 512), shape(512, 1024)]
    outs += [shape(rows, 512), jax.ShapeDtypeStruct((4, 8, rows), f32)]
    return staged(body, "forward_cross", head, [(own, EARLY, EARLY + MIDDLE), (other, EARLY, EARLY + MIDDLE), low, mem, mem2, qa, ka], outs)


LAST = 1920


def backward(
    head, cross_q, mem_kv, cross_qa, cross_ka, cross_mix, cross_lse, cross_grad, w_query, resid_grad, norms, w_out,
    tok, mix, q, kv, qa, ka, lse, tok2, mem, mem2, low, norm_grads,
):
    rows = tok.shape[0]
    values = [cross_q, mem_kv, cross_qa, cross_ka, cross_mix, cross_lse, cross_grad, w_query, resid_grad, norms, w_out]
    values += [tok, mix, q, kv, qa, ka, lse, tok2, mem, mem2, low, norm_grads]

    def body(core, get, made, put, dkt, dvt, dq_cross, branch, mix_grad):
        keep, send, resid_out, dk_c, dk2_c, dv_c, dv2_c, dq, dk, dk2, dv, dv2 = made
        attention_back(*[get(i) for i in range(7)], dq_cross, dk_c, dk2_c, dv_c, dv2_c, dkt, dvt)
        for i in (4, 6, 3, 5):
            put(i)
        w_query, resid_grad, norms, w_out, tok, mix = [get(i) for i in range(7, 13)]
        size = rows // 2
        sums = [jnp.zeros((1, 512), f32) for _ in range(2)]
        for block in range(2):
            here = slice(block * size, block * size + size)
            resid = tok[here, :].astype(f32) + mm(mix[here, :], w_out[...])
            _, normed, inverse = norm(resid, norms[0:1, :], norms[3:4, :])
            grad = resid_grad[here, :] + mm(dq_cross[here, :], w_query[...], NT)
            sums[0] += jnp.sum(grad * normed, 0, keepdims=True)
            sums[1] += jnp.sum(grad, 0, keepdims=True)
            grad = norm_back(grad, normed, inverse, norms[0:1, :])
            resid_out[here, :] = grad
            branch[here, :] = grad.astype(bf16)
            mix_grad[here, :] = mm(branch[here, :], w_out[...], NT).astype(bf16)
        put(2)
        attention_back(get(13), get(14), get(15), get(16), mix, get(17), mix_grad, dq, dk, dk2, dv, dv2, dkt, dvt)
        for i in (9, 11, 7, 8, 10):
            put(i)

        tok2, mem, mem2, low, norm_grads = [get(i) for i in range(18, 23)]
        sides = (core, 1 - core)
        columns = [pl.ds(pl.multiple_of(side * 256, 256), 256) for side in sides]

        def store(slot, *pairs):
            for target, here in zip((keep, send), columns):
                value = sum(mm(left, right[:, here]) for left, right in pairs)
                target[:, 256 * slot : 256 * slot + 256] = value.astype(bf16)

        blank = jnp.zeros((1, 512), f32)
        every = jnp.concatenate([sums[0], norm_grads[0:2, :], blank, sums[1], norm_grads[2:4, :], blank], 0)
        padded = jnp.concatenate([in_fours(every), jnp.zeros((120, 512), f32)], 0).T.astype(bf16)
        for target in (keep, send):
            target[:, 1792:] = padded
        store(4, (low[...].T, dq_cross))
        store(3, (mix[...].T, branch))
        near, far = mem[...].T, mem2[...].T
        store(5, (near, dk_c), (far, dk2_c))
        store(6, (near, dv_c), (far, dv2_c))
        near, far = tok[...].T, tok2[...].T
        store(0, (near, dq))
        store(1, (near, dk), (far, dk2))
        store(2, (near, dv), (far, dv2))
        put(1)
        put(0)

    outs = [shape(512, LAST), shape(512, LAST), shape(rows, 512, f32)] + [shape(rows, 512)] * 9
    scratch = [pltpu.VMEM((128, 2 * rows), f32)] * 2 + [pltpu.VMEM((rows, 512), bf16)] * 3
    return staged(body, "backward", head, values, outs, scratch)


def finish(head, third, other_third, same, slot, dk, dk2, dv, dv2, w_kv, grad, dq, dsk, dsk2, dsv, dsv2, w_self):
    rows = third.shape[0]

    def body(core, get, made, put):
        out, grad_memory, grad_tokens = made
        third, slot = get(0), get(3)
        size = rows // 2
        ahead = jnp.concatenate([mm(third[...], slot[512:, :])[1:, :], mm(get(1)[...], slot[512:, :])[:1, :]], 0)
        out[...] = (mm(third[...], slot[:512, :]) + ahead * get(2)[:, :1]).astype(bf16)
        put(0)

        def summed(a, b, here):
            return (get(a)[here, :].astype(f32) + get(b)[here, :].astype(f32)).astype(bf16)

        for block in range(2):
            here = pl.ds(block * size, size)
            grad_memory[here, :] = mm(summed(4, 5, here), get(8)[:, :512], NT) + mm(
                summed(6, 7, here), get(8)[:, 512:], NT
            )
        put(1)
        for block in range(2):
            here = pl.ds(block * size, size)
            w_self = get(15)
            value = get(9)[here, :] + mm(get(10)[here, :], w_self[:, :512], NT)
            value = value + mm(summed(11, 12, here), w_self[:, 512:1024], NT)
            grad_tokens[here, :] = value + mm(summed(13, 14, here), w_self[:, 1024:], NT)
        put(2)

    values = [third, other_third, same, slot, dk, dk2, dv, dv2, w_kv, grad, dq, dsk, dsk2, dsv, dsv2, w_self]
    outs = [shape(rows, 512), shape(rows, 512, f32), shape(rows, 512, f32)]
    return staged(body, "finish", head, values, outs)


def one_hot(rows, columns, target):
    row = lax.broadcasted_iota(jnp.int32, (rows, columns), 0)
    column = lax.broadcasted_iota(jnp.int32, (rows, columns), 1)
    return jnp.where(target(row) == column, 1.0, 0.0).astype(bf16)


def spread_units(row):
    return ((row >> 3) & 3) * 128 + (row >> 5) * 8 + (row & 7)


def spread_rows(row):
    return ((row >> 3) & 1) * 256 + (row >> 4) * 8 + (row & 7)


def norm(resid, gain, bias):
    center = resid - jnp.mean(resid, -1, keepdims=True)
    inverse = lax.rsqrt(jnp.mean(center * center, -1, keepdims=True) + epsilon)
    normed = center * inverse
    return normed * gain + bias, normed, inverse


def norm_back(upstream, normed, inverse, gain):
    scaled = upstream * gain
    mean = jnp.mean(scaled, -1, keepdims=True)
    slope = jnp.mean(scaled * normed, -1, keepdims=True)
    return inverse * (scaled - mean - normed * slope)


def gelu(v):
    root = 0.7978845608028654
    square = v * v
    t = jnp.tanh(root * (v + 0.044715 * square * v))
    up = 0.5 * (1.0 + t)
    return v * up, up + 0.5 * v * (1.0 - t * t) * (root * (1.0 + 3 * 0.044715 * square))


def forward_back_body(
    size, core, get, made, put,
    w_in, w_out, w_cross, hidden_t, inner_grad, second_t, branch_three, branch_two, third_t,
):
    third_out, slot, keep, send, resid_grad, mix_grad, norm_grads = made
    own, other = get(0), get(1)
    rows = third_out.shape[0]

    def packed(side, here, lanes):
        return jnp.where(core == side, own[here, lanes], other[here, lanes])

    units = one_hot(512, 512, spread_units)
    every = slice(0, 512)
    for chunk in range(4):
        start = 512 * (chunk % 2)
        moved = mm(packed(chunk // 2, every, slice(start, start + 512)), units).astype(bf16)
        for k in range(4):
            w_in[:, 512 * k + 128 * chunk : 512 * k + 128 * chunk + 128] = moved[:, 128 * k : 128 * k + 128]
    for k in range(4):
        for side in range(2):
            w_out[512 * k : 512 * k + 512, 256 * side : 256 * side + 256] = packed(
                side, every, slice(OUT + 256 * k, OUT + 256 + 256 * k)
            )
    for side in range(2):
        w_cross[:, 256 * side : 256 * side + 256] = packed(side, every, slice(CROSS, CROSS + 256))
    order = one_hot(512, 512, spread_rows)
    for side in range(2):
        for level in range(2):
            here = slice(256 * level, 256 * level + 256)
            stack = jnp.concatenate([packed(side, here, slice(SLOT + 256 * k, SLOT + 256 + 256 * k)) for k in range(2)], 0)
            slot[512 * level : 512 * level + 512, 256 * side : 256 * side + 256] = mm(order, stack).astype(bf16)
    put(1)
    mix, first, norms, cot, cot_behind = [get(i) for i in range(2, 7)]
    gain_two, gain_three = norms[1:2, :], norms[2:3, :]
    bias_two, bias_three = norms[4:5, :], norms[5:6, :]
    sums = [jnp.zeros((1, 512), f32) for _ in range(4)]
    for block in range(rows // size):
        here = slice(block * size, block * size + size)
        resid = first[here, :] + mm(mix[here, :], w_cross[...])
        second_block, normed_two, inverse_two = norm(resid, gain_two, bias_two)
        second_low = second_block.astype(bf16)
        second_t[:, here] = second_low.T
        resid = second_block
        slopes = []
        for k in range(4):
            part = slice(512 * k, 512 * k + 512)
            value, slope = gelu(mm(second_low, w_in[:, part]))
            value = value.astype(bf16)
            hidden_t[part, here] = value.T
            slopes.append(slope)
            resid = resid + mm(value, w_out[part, :])
        third, normed_three, inverse_three = norm(resid, gain_three, bias_three)
        third_low = third.astype(bf16)
        third_out[here, :] = third_low
        third_t[:, here] = mm(third_low, order, NN).astype(bf16).T
        grad = mm(cot[here, :], slot[:512, :], NT) + mm(cot_behind[here, :], slot[512:, :], NT)
        sums[1] += jnp.sum(grad * normed_three, 0, keepdims=True)
        sums[3] += jnp.sum(grad, 0, keepdims=True)
        grad = norm_back(grad, normed_three, inverse_three, gain_three)
        branch = grad.astype(bf16)
        branch_three[here, :] = branch
        for k in range(4):
            part = slice(512 * k, 512 * k + 512)
            inner = (mm(branch, w_out[part, :], NT) * slopes[k]).astype(bf16)
            inner_grad[here, part] = inner
            grad = grad + mm(inner, w_in[:, part], NT)
        sums[0] += jnp.sum(grad * normed_two, 0, keepdims=True)
        sums[2] += jnp.sum(grad, 0, keepdims=True)
        grad = norm_back(grad, normed_two, inverse_two, gain_two)
        resid_grad[here, :] = grad
        branch = grad.astype(bf16)
        branch_two[here, :] = branch
        mix_grad[here, :] = mm(branch, w_cross[...], NT).astype(bf16)
    norm_grads[...] = jnp.concatenate(sums + [jnp.zeros((4, 512), f32)], 0)
    for i in (0, 4, 5, 6):
        put(i)

    mix_t = mix[...].T
    for which, target, side in ((3, send, 1 - core), (2, keep, core)):
        columns = pl.ds(pl.multiple_of(side * 256, 256), 256)
        near, behind = cot[:, columns], cot_behind[:, columns]
        for k in range(2):
            lanes = slice(SLOT + 256 * k, SLOT + 256 + 256 * k)
            target[:256, lanes] = mm(third_t[256 * k : 256 * k + 256, :], near).astype(bf16)
            target[256:, lanes] = mm(third_t[256 * k : 256 * k + 256, :], behind).astype(bf16)
        target[:, CROSS : CROSS + 256] = mm(mix_t, branch_two[:, columns]).astype(bf16)
        for k in range(4):
            value = mm(hidden_t[512 * k : 512 * k + 512, :], branch_three[:, columns])
            target[:, OUT + 256 * k : OUT + 256 + 256 * k] = value.astype(bf16)
        for chunk in range(2):
            starts = [pl.multiple_of(512 * k + 256 * side + 128 * chunk, 128) for k in range(4)]
            pieces_here = [inner_grad[:, pl.ds(start, 128)] for start in starts]
            grad = mm(second_t[...], jnp.concatenate(pieces_here, 1)).astype(bf16)
            target[:, 512 * chunk : 512 * chunk + 512] = mm(grad, units, NT).astype(bf16)
        put(which)


def forward_back(head, own, other, mix, first, norms, cot, cot_behind, size=384):
    rows = mix.shape[0]
    outs = [shape(rows, 512), shape(1024, 512), shape(512, LATE), shape(512, LATE)]
    outs += [shape(rows, 512, f32), shape(rows, 512), shape(8, 512, f32)]
    scratch = [pltpu.VMEM((512, 2048), bf16), pltpu.VMEM((2048, 512), bf16), pltpu.VMEM((512, 512), bf16)]
    scratch += [pltpu.VMEM((2048, rows), bf16), pltpu.VMEM((rows, 2048), bf16), pltpu.VMEM((512, rows), bf16)]
    scratch += [pltpu.VMEM((rows, 512), bf16)] * 2 + [pltpu.VMEM((512, rows), bf16)]
    body = functools.partial(forward_back_body, size)
    return staged(body, "forward_back", head, [own, other, mix, first, norms, cot, cot_behind], outs, scratch)


def combined(keep, arrived):
    return (keep.astype(f32) + arrived.astype(f32)).astype(bf16).reshape(64, 8, keep.shape[1])


def to_owners(mine):
    return lax.all_to_all(mine, "dp", split_axis=0, concat_axis=0, tiled=True)


def owned(sums):
    core = lax.axis_index("head")
    mine = lax.dynamic_slice_in_dim(sums, core * 4, 4, 0)
    other = swap(lax.dynamic_slice_in_dim(sums, 4 - core * 4, 4, 0))
    return mine, other


def joined(mine, other, *slots):
    return jnp.concatenate([by_core(mine[:, s : s + 256], other[:, s : s + 256], 1) for s in slots], 1)


def shards(
    tokens,
    memory,
    segments,
    mem_segments,
    cotangent,
    self_proj,
    self_output,
    cross_query,
    cross_keyval,
    cross_output,
    hidden_in,
    hidden_out,
    slot_proj,
    norm_gain,
    norm_bias,
):
    rows = tokens.shape[0]
    core = lax.axis_index("head")
    head = core.astype(jnp.int32).reshape(1, 1)

    def spread(mine):
        block = jnp.broadcast_to(mine[None], (64,) + mine.shape)
        block = lax.all_to_all(block, "dp", split_axis=0, concat_axis=0, tiled=True)
        return block.reshape(512, mine.shape[1])

    norms = jnp.pad(jnp.concatenate([norm_gain, norm_bias], 1), ((0, 1), (0, 120)))
    mine, sent = halves(
        self_proj[:, 0], self_proj[:, 1], self_proj[:, 2], self_output, jnp.concatenate([norms, norms], 1),
        cross_query, cross_keyval[:, 0], cross_keyval[:, 1],
    )
    early = by_core(mine, swap(sent), 0)
    early, segments, mem_segments, cotangent, hidden_in, hidden_out, slot_proj = tie(
        early, segments, mem_segments, cotangent, hidden_in, hidden_out, slot_proj
    )
    early = spread(early)
    late_mine, late_sent = halves(hidden_in, cross_output)
    tall, tall_sent = halves(hidden_out[:8], hidden_out[8:], slot_proj)
    tall_other = swap(tall_sent)
    late = by_core(late_mine, swap(late_sent), 0)
    tall = [by_core(tall[:, :512], tall_other[:, :512], 1), by_core(tall[:, 512:], tall_other[:, 512:], 1)]
    late = jnp.concatenate([late] + tall, 1)

    other_tokens, other_memory = swap(tokens), swap(memory)
    other_seg, other_mem_seg = swap(segments), swap(mem_segments)
    other_cot = swap(cotangent[-1:])
    self_qa, self_ka = extras(segments, jnp.concatenate([segments, other_seg]))
    cross_qa, cross_ka = extras(segments, jnp.concatenate([mem_segments, other_mem_seg]))
    before = jnp.concatenate([jnp.where(core == 1, other_seg[-1:], -1), segments[:-1]])
    after = jnp.concatenate([segments[1:], jnp.where(core == 0, other_seg[:1], -1)])
    cot_behind = jnp.where((before == segments)[:, None], jnp.concatenate([other_cot, cotangent[:-1]]), bf16(0))
    same_after = jnp.broadcast_to((after == segments)[:, None], (rows, 128)).astype(f32)

    early, late, cot_behind, self_qa, self_ka, cross_qa, cross_ka, same_after = tie(
        early, late, cot_behind, self_qa, self_ka, cross_qa, cross_ka, same_after
    )
    early_other = swap(early)
    late = spread(late)

    query, keyval, w_self, w_out, norms, self_mix, self_lse, first, first_low = forward_self(
        head, early, early_other, tokens, other_tokens, self_qa, self_ka
    )
    cross_q, mem_keyval, w_query, w_kv, cross_mix, cross_lse = forward_cross(
        head, early, early_other, first_low, memory, other_memory, cross_qa, cross_ka
    )
    late, cross_mix = tie(late, cross_mix)
    third_low, slot, keep, send, grad_resid, grad_cross_mix, norm_grads = forward_back(
        head, late, swap(late), cross_mix, first, norms, cotangent, cot_behind
    )
    other_third = swap(third_low[:1])
    keep, grad_cross_mix = tie(combined(keep, swap(send)), grad_cross_mix)
    late_sums = to_owners(keep)

    keep, send, grad_resid, dk_cross, dk2_cross, dv_cross, dv2_cross, dq, dk, dk2, dv, dv2 = backward(
        head, cross_q, mem_keyval, cross_qa, cross_ka, cross_mix, cross_lse, grad_cross_mix, w_query, grad_resid, norms,
        w_out, tokens, self_mix, query, keyval, self_qa, self_ka, self_lse, other_tokens, memory, other_memory,
        first_low, norm_grads,
    )
    arrived = swap(send)
    other_keys = [swap(v) for v in (dk2_cross, dv2_cross, dk2, dv2)]
    mine, late_sums, third_low, other_third, *other_keys = tie(
        combined(keep, arrived), late_sums, third_low, other_third, *other_keys
    )
    last_sums = to_owners(mine)

    sums = jnp.sum(late_sums.astype(f32), 0)
    mine, other = owned(sums[:, :OUT])
    tall = [
        jnp.concatenate([half(sums[:, OUT:SLOT], c), half(sums[:, SLOT:], c)], 1) for c in (core, 1 - core)
    ]
    tall, tall_other = tall[0], swap(tall[1])
    out, grad_memory, grad_tokens = finish(
        head, third_low, jnp.broadcast_to(other_third, (16, 512)), same_after, slot,
        dk_cross, other_keys[0], dv_cross, other_keys[1], w_kv, grad_resid, dq, dk, other_keys[2], dv, other_keys[3], w_self,
    )
    g_hidden_in = by_core(mine[:, :1024], other[:, :1024], 1)
    g_hidden_out = jnp.concatenate([joined(tall, tall_other, 0), joined(tall, tall_other, 256)])
    g_slot = joined(tall, tall_other, 512)
    out, grad_memory, grad_tokens, last_sums = tie(out, grad_memory, grad_tokens, last_sums)
    last, last_other = owned(jnp.sum(last_sums.astype(f32), 0))
    return (
        out,
        grad_tokens,
        grad_memory,
        joined(last, last_other, 0, 256, 512).reshape(4, 3, 512),
        joined(last, last_other, 768),
        joined(last, last_other, 1024),
        joined(last, last_other, 1280, 1536).reshape(4, 2, 512),
        joined(mine, other, 1024),
        g_hidden_in,
        g_hidden_out,
        g_slot,
        last[:3, 1792:1796],
        last[:3, 1796:1800],
    )


def solution(mesh):
    split = P(ALL, None)
    cube = P(ALL, None, None)
    flat = P(ALL)
    columns = P(None, ALL)
    in_specs = (split, split, flat, flat, split, cube, split, split, cube, split, split, split, split, columns, columns)
    out_specs = (split, split, split, cube, split, split, cube, split, split, split, split, columns, columns)
    return jax.shard_map(shards, mesh=mesh, in_specs=in_specs, out_specs=out_specs, check_vma=False)
```

```python
import functools

import jax
import jax.numpy as jnp
from jax import lax
from jax.experimental import pallas as pl
from jax.experimental.pallas import tpu as pltpu
from jax.sharding import PartitionSpec as P

HEAD_DIM = 64
epsilon = 1e-05
f32 = jnp.float32
bf16 = jnp.bfloat16
ALL = ("dp", "head")
NT = (((1,), (1,)), ((), ()))
NN = (((1,), (0,)), ((), ()))
TN = (((0,), (0,)), ((), ()))
blocked = -1e30


def mm(a, b, dims=NN):
    return lax.dot_general(a, b, dims, preferred_element_type=f32)


def low_half(shape):
    return lax.broadcasted_iota(jnp.int32, shape, 1) < HEAD_DIM


def pieces(x):
    hi = x.astype(bf16)
    rest = x - hi.astype(f32)
    mid = rest.astype(bf16)
    return hi, mid, (rest - mid.astype(f32)).astype(bf16)


def attention(q_ref, kv_ref, qa_ref, ka_ref, o_ref, lse_ref, size=768):
    rows, width = q_ref.shape
    total = kv_ref.shape[0]

    def pair(p):
        here = slice(128 * p, 128 * p + 128)
        key_low = low_half((total, 128))
        keys, key_extra = kv_ref[:, here], ka_ref[...]
        key_tiles = [jnp.where(key_low, keys, key_extra), jnp.where(key_low, key_extra, keys)]
        turned = kv_ref[:, slice(128 * p + width, 128 * p + width + 128)].T
        ones = jnp.ones((16, total), bf16)
        value_tiles = [jnp.concatenate([turned[64 * h : 64 * h + 64], ones], 0) for h in range(2)]
        low = low_half((size, 128))
        for block in range(rows // size):
            span = slice(block * size, block * size + size)
            q = q_ref[span, here] * bf16(HEAD_DIM**-0.5)
            qa = qa_ref[span, :]
            outs, sums = [], []
            for h in range(2):
                q_tile = jnp.where(low, q, qa) if h == 0 else jnp.where(low, qa, q)
                scores = mm(key_tiles[h], q_tile, NT)
                peak = jnp.max(scores, 0, keepdims=True)
                mixed = mm(value_tiles[h], jnp.exp(scores - peak).astype(bf16))
                count = mixed[64:65, :]
                outs.append(mixed[:64, :] * (1.0 / count))
                sums.append(peak + jnp.log(count))
            o_ref[span, here] = jnp.concatenate(outs, 0).T.astype(bf16)
            lse_ref[p, :, span] = jnp.concatenate(sums + [jnp.zeros((6, size), f32)], 0)

    for p in range(width // 128):
        pair(p)


def attention_back(
    q_ref, kv_ref, qa_ref, ka_ref, o_ref, lse_ref, do_ref, dq_ref, dk_ref, dk2_ref, dv_ref, dv2_ref, dkt, dvt, size=384
):
    rows, width = q_ref.shape
    total = kv_ref.shape[0]

    def pair(p, carry):
        lanes = pl.ds(pl.multiple_of(128 * p, 128), 128)
        key_low = low_half((total, 128))
        keys, key_extra = kv_ref[:, lanes], ka_ref[...]
        values = kv_ref[:, pl.ds(pl.multiple_of(128 * p + width, 128), 128)]
        ones = jnp.ones_like(values)
        key_tiles = [jnp.where(key_low, keys, key_extra), jnp.where(key_low, key_extra, keys)]
        value_tiles = [jnp.where(key_low, values, ones), jnp.where(key_low, ones, values)]
        low = low_half((size, 128))
        lane = lax.broadcasted_iota(jnp.int32, (size, 128), 1)
        lse_columns = lse_ref[p].T
        for block in range(rows // size):
            here = slice(block * size, block * size + size)
            q = q_ref[here, lanes] * bf16(HEAD_DIM**-0.5)
            qa = qa_ref[here, :]
            do = do_ref[here, lanes]
            product = do.astype(f32) * o_ref[here, lanes].astype(f32)
            lse = lse_columns[here, :]
            q_turned, do_turned = q.T, do.T
            dqs = []
            for h in range(2):
                spare = HEAD_DIM * (1 - h)
                mine = low if h == 0 else jnp.logical_not(low)
                delta = jnp.sum(jnp.where(mine, product, 0.0), -1, keepdims=True)
                d0, d1, d2 = pieces(-delta)
                l0, l1, l2 = pieces(-lse[:, h : h + 1])
                q_extra = jnp.where(
                    lane == spare + 3, l0, jnp.where(lane == spare + 4, l1, jnp.where(lane == spare + 5, l2, qa))
                )
                do_extra = jnp.where(
                    lane == spare, d0, jnp.where(lane == spare + 1, d1, jnp.where(lane == spare + 2, d2, bf16(0)))
                )
                probs = jnp.exp(mm(jnp.where(mine, q, q_extra), key_tiles[h], NT))
                grad = mm(jnp.where(mine, do, do_extra), value_tiles[h], NT)
                low_probs = probs.astype(bf16)
                ds = (probs * grad).astype(bf16)
                dqs.append(mm(ds, keys))
                part = slice(HEAD_DIM * h, HEAD_DIM * h + HEAD_DIM)
                new_dk = mm(q_turned[part, :], ds)
                new_dv = mm(do_turned[part, :], low_probs)
                if block == 0:
                    dkt[part, :] = new_dk
                    dvt[part, :] = new_dv
                else:
                    dkt[part, :] += new_dk
                    dvt[part, :] += new_dv
            dq_ref[here, lanes] = (jnp.where(low, dqs[0], dqs[1]) * HEAD_DIM**-0.5).astype(bf16)
        for turned, near, far in ((dkt, dk_ref, dk2_ref), (dvt, dv_ref, dv2_ref)):
            near[:, lanes] = turned[:, :rows].astype(bf16).T
            far[:, lanes] = turned[:, rows:].astype(bf16).T
        return carry

    lax.fori_loop(0, width // 128, pair, 0)


def swap(value):
    return lax.ppermute(value, "head", [(0, 1), (1, 0)])


def tie(*values):
    return lax.optimization_barrier(values)


def by_core(own, other, axis):
    first = lax.axis_index("head") == 0
    return jnp.where(first, jnp.concatenate([own, other], axis), jnp.concatenate([other, own], axis))


def half(value, core):
    width = value.shape[-1] // 2
    return lax.dynamic_slice_in_dim(value, core * width, width, value.ndim - 1)


def halves(*weights):
    sides = [jnp.concatenate([w[:, w.shape[1] // 2 * i : w.shape[1] // 2 * (i + 1)] for w in weights], 1) for i in (0, 1)]
    first = lax.axis_index("head") == 0
    return jnp.where(first, sides[0], sides[1]), jnp.where(first, sides[1], sides[0])


EARLY = 1152
MIDDLE = 768
LATE = 2816
CROSS, OUT, SLOT = 1024, 1280, 2304


def staged(body, name, head, values, outs, scratch=(), order=None, limit=60):
    count, results = len(values), len(outs)
    spans = [v[1:] if isinstance(v, tuple) else None for v in values]
    values = [v[0] if isinstance(v, tuple) else v for v in values]
    sizes = [v.shape if span is None else (v.shape[0], span[1] - span[0]) for v, span in zip(values, spans)]

    def kernel(*refs):
        head_ref, sources, targets = refs[0], refs[1 : 1 + count], refs[1 + count : 1 + count + results]
        rest = refs[1 + count + results :]
        inside, made = rest[:count], rest[count : count + results]
        in_sems, out_sems = rest[count + results], rest[count + results + 1]
        loads = []
        for i in range(count):
            source = sources[i] if spans[i] is None else sources[i].at[:, spans[i][0] : spans[i][1]]
            loads.append(pltpu.make_async_copy(source, inside[i], in_sems.at[i]))
        for i in order or range(count):
            loads[i].start()
        waited, stores = set(), []

        def get(i):
            if i not in waited:
                loads[i].wait()
                waited.add(i)
            return inside[i]

        def put(i):
            store = pltpu.make_async_copy(made[i], targets[i], out_sems.at[i])
            store.start()
            stores.append(store)

        body(head_ref[0, 0], get, made, put, *rest[count + results + 2 :])
        for i in range(count):
            get(i)
        for store in stores:
            store.wait()

    return pl.pallas_call(
        kernel,
        in_specs=[pl.BlockSpec(memory_space=pltpu.SMEM)] + [pl.BlockSpec(memory_space=pltpu.HBM)] * count,
        out_specs=[pl.BlockSpec(memory_space=pltpu.HBM)] * results,
        out_shape=outs,
        scratch_shapes=[pltpu.VMEM(size, v.dtype) for size, v in zip(sizes, values)]
        + [pltpu.VMEM(o.shape, o.dtype) for o in outs]
        + [pltpu.SemaphoreType.DMA((count,)), pltpu.SemaphoreType.DMA((results,))]
        + list(scratch),
        compiler_params=pltpu.CompilerParams(vmem_limit_bytes=limit * 2**20),
        name=name,
    )(head, *values)


def in_fours(rows):
    place = lax.broadcasted_iota(jnp.int32, (1, 512), 1) & 3
    moved = {s: pltpu.roll(rows, s % 512, 1) for s in range(-3, 4)}
    made = []
    for base in (0, 4):
        for c in range(4):
            row = jnp.zeros((1, 512), f32)
            for n in range(4):
                row = row + jnp.where(place == n, moved[n - c][base + n : base + n + 1, :], 0.0)
            made.append(row)
    return jnp.concatenate(made, 0)


def shape(rows, columns, kind=bf16):
    return jax.ShapeDtypeStruct((rows, columns), kind)


def prepare(head, own, other, mem, mem2):
    rows = own.shape[0]

    def body(core, get, made, put):
        qa, ka, cross_ka, same = made
        segs = [get(i)[...].astype(f32).reshape(1, rows) for i in range(4)]
        segs = jnp.concatenate(segs + [jnp.zeros((4, rows), f32)], 0)
        lane = lax.broadcasted_iota(jnp.int32, (rows, 128), 1) & 63
        marks, ones = lane < 3, (lane >= 3) & (lane < 6)
        number = lane.astype(f32)
        columns = segs.T
        qa[...] = jnp.where(marks & (columns[:, 0:1] != number), blocked, 0.0).astype(bf16)
        for target, first in ((ka, 0), (cross_ka, 2)):
            for i in range(2):
                match = (marks & (columns[:, first + i : first + i + 1] == number)) | ones
                target[rows * i : rows * i + rows, :] = jnp.where(match, 1.0, 0.0).astype(bf16)
        place = lax.broadcasted_iota(jnp.int32, (1, rows), 1)
        down, up = pltpu.roll(segs, 1, 1), pltpu.roll(segs, rows - 1, 1)
        last = jnp.where(core == 1, down[1:2, :], -1.0)
        next_one = jnp.where(core == 0, up[1:2, :], -1.0)
        same_down = jnp.where(jnp.where(place == 0, last, down[0:1, :]) == segs[0:1, :], 1.0, 0.0)
        same_up = jnp.where(jnp.where(place == rows - 1, next_one, up[0:1, :]) == segs[0:1, :], 1.0, 0.0)
        columns = jnp.concatenate([same_down, same_up, jnp.zeros((6, rows), f32)], 0).T
        lane = lax.broadcasted_iota(jnp.int32, (rows, 128), 1)
        same[...] = jnp.where(lane == 0, columns[:, 0:1], columns[:, 1:2])
        for i in range(4):
            put(i)

    outs = [shape(rows, 128), shape(2 * rows, 128), shape(2 * rows, 128), shape(rows, 128, f32)]
    return staged(body, "prepare", head, [own, other, mem, mem2], outs)


def shift_down(head, cot, far, same):
    rows = cot.shape[0]

    def body(core, get, made, put):
        (behind,) = made
        moved = pltpu.roll(get(0)[...].astype(f32), 1, 0)
        row = lax.broadcasted_iota(jnp.int32, (rows, 512), 0)
        moved = jnp.where(row == 0, get(1)[...].astype(f32)[15:16, :], moved)
        behind[...] = jnp.where(get(2)[:, 0:1] > 0.0, moved, 0.0).astype(bf16)
        put(0)

    return staged(body, "shift_down", head, [cot, far, same], [shape(rows, 512)])[0]


def spread_kernel(block, out):
    out[...] = jnp.broadcast_to(block[...][None], out.shape)


def spread_early(block):
    return pl.pallas_call(
        spread_kernel,
        grid=(8,),
        in_specs=[pl.BlockSpec(block.shape, lambda i: (0, 0))],
        out_specs=pl.BlockSpec((8,) + block.shape, lambda i: (i, 0, 0)),
        out_shape=jax.ShapeDtypeStruct((64,) + block.shape, bf16),
        name="spread_early",
    )(block)


def both_halves(core, own, other, slot):
    here = slice(256 * slot, 256 * slot + 256)
    a, b = own[:, here], other[:, here]
    return jnp.concatenate([jnp.where(core == 0, a, b), jnp.where(core == 0, b, a)], 1)


def forward_self(head, own, other, tok, tok2, qa, ka):
    rows = tok.shape[0]

    def body(core, get, made, put):
        q, kv, w_self, w_out, norms, mix, lse, first, low = made
        own, other = get(0), get(1)
        for part in range(3):
            w_self[:, 512 * part : 512 * part + 512] = both_halves(core, own, other, part)
        put(2)
        q[...] = mm(get(2)[...], w_self[:, :512]).astype(bf16)
        put(0)
        kv[:rows, :] = mm(get(2)[...], w_self[:, 512:]).astype(bf16)
        kv[rows:, :] = mm(get(3)[...], w_self[:, 512:]).astype(bf16)
        put(1)
        w_out[...] = both_halves(core, own, other, 3)
        put(3)
        turned = in_fours(own[:, 1024:].astype(f32).T[:8, :])
        norms[...] = jnp.concatenate([turned[:3, :], turned[4:7, :], jnp.zeros((2, 512), f32)], 0)
        put(4)
        attention(q, kv, get(4), get(5), mix, lse)
        put(5)
        put(6)
        size = rows // 2
        for block in range(2):
            here = slice(block * size, block * size + size)
            value = get(2)[here, :].astype(f32) + mm(mix[here, :], w_out[...])
            value = norm(value, norms[0:1, :], norms[3:4, :])[0]
            first[here, :] = value
            low[here, :] = value.astype(bf16)
        put(8)
        put(7)

    outs = [shape(rows, 512), shape(2 * rows, 1024), shape(512, 1536), shape(512, 512), shape(8, 512, f32)]
    outs += [shape(rows, 512), jax.ShapeDtypeStruct((4, 8, rows), f32), shape(rows, 512, f32), shape(rows, 512)]
    return staged(body, "forward_self", head, [(own, 0, EARLY), (other, 0, EARLY), tok, tok2, qa, ka], outs)


def forward_cross(head, own, other, low, mem, mem2, qa, ka):
    rows = mem.shape[0]

    def body(core, get, made, put):
        q, kv, w_query, w_kv, mix, lse = made
        own, other = get(0), get(1)
        w_query[...] = both_halves(core, own, other, 0)
        w_kv[:, :512] = both_halves(core, own, other, 1)
        w_kv[:, 512:] = both_halves(core, own, other, 2)
        put(2)
        put(3)
        q[...] = mm(get(2)[...], w_query[...]).astype(bf16)
        put(0)
        kv[:rows, :] = mm(get(3)[...], w_kv[...]).astype(bf16)
        kv[rows:, :] = mm(get(4)[...], w_kv[...]).astype(bf16)
        put(1)
        attention(q, kv, get(5), get(6), mix, lse)
        put(4)
        put(5)

    outs = [shape(rows, 512), shape(2 * rows, 1024), shape(512, 512), shape(512, 1024)]
    outs += [shape(rows, 512), jax.ShapeDtypeStruct((4, 8, rows), f32)]
    return staged(body, "forward_cross", head, [(own, EARLY, EARLY + MIDDLE), (other, EARLY, EARLY + MIDDLE), low, mem, mem2, qa, ka], outs)


LAST = 1920


def backward(
    head, cross_q, mem_kv, qa_first, cross_ka, cross_mix, cross_lse, cross_grad, w_query, resid_grad, norms, w_out,
    tok, mix, q, kv, qa, ka, lse, tok2, mem, mem2, low, norm_grads,
):
    rows = tok.shape[0]
    values = [cross_q, mem_kv, qa_first, cross_ka, cross_mix, cross_lse, cross_grad, w_query, resid_grad, norms, w_out]
    values += [tok, mix, q, kv, qa, ka, lse, tok2, mem, mem2, low, norm_grads]

    def body(core, get, made, put, dkt, dvt, dq_cross, branch, mix_grad):
        keep, send, resid_out, dk_c, dk2_c, dv_c, dv2_c, dq, dk, dk2, dv, dv2 = made
        attention_back(*[get(i) for i in range(7)], dq_cross, dk_c, dk2_c, dv_c, dv2_c, dkt, dvt)
        for i in (4, 6, 3, 5):
            put(i)
        w_query, resid_grad, norms, w_out, tok, mix = [get(i) for i in range(7, 13)]
        size = rows // 2
        sums = [jnp.zeros((1, 512), f32) for _ in range(2)]
        for block in range(2):
            here = slice(block * size, block * size + size)
            resid = tok[here, :].astype(f32) + mm(mix[here, :], w_out[...])
            _, normed, inverse = norm(resid, norms[0:1, :], norms[3:4, :])
            grad = resid_grad[here, :] + mm(dq_cross[here, :], w_query[...], NT)
            sums[0] += jnp.sum(grad * normed, 0, keepdims=True)
            sums[1] += jnp.sum(grad, 0, keepdims=True)
            grad = norm_back(grad, normed, inverse, norms[0:1, :])
            resid_out[here, :] = grad
            branch[here, :] = grad.astype(bf16)
            mix_grad[here, :] = mm(branch[here, :], w_out[...], NT).astype(bf16)
        put(2)
        attention_back(get(13), get(14), get(15), get(16), mix, get(17), mix_grad, dq, dk, dk2, dv, dv2, dkt, dvt)
        for i in (9, 11, 7, 8, 10):
            put(i)

        tok2, mem, mem2, low, norm_grads = [get(i) for i in range(18, 23)]
        sides = (core, 1 - core)
        columns = [pl.ds(pl.multiple_of(side * 256, 256), 256) for side in sides]

        jobs = []

        def store(slot, *pairs):
            jobs.append((slot, pairs))

        blank = jnp.zeros((1, 512), f32)
        every = jnp.concatenate([sums[0], norm_grads[0:2, :], blank, sums[1], norm_grads[2:4, :], blank], 0)
        padded = jnp.concatenate([in_fours(every), jnp.zeros((120, 512), f32)], 0).T.astype(bf16)
        for target in (keep, send):
            target[:, 1792:] = padded
        store(4, (low[...].T, dq_cross))
        store(3, (mix[...].T, branch))
        near, far = mem[...].T, mem2[...].T
        store(5, (near, dk_c), (far, dk2_c))
        store(6, (near, dv_c), (far, dv2_c))
        near, far = tok[...].T, tok2[...].T
        store(0, (near, dq))
        store(1, (near, dk), (far, dk2))
        store(2, (near, dv), (far, dv2))
        for which, target, here in ((1, send, columns[1]), (0, keep, columns[0])):
            for slot, pairs in jobs:
                value = sum(mm(left, right[:, here]) for left, right in pairs)
                target[:, 256 * slot : 256 * slot + 256] = value.astype(bf16)
            put(which)

    outs = [shape(512, LAST), shape(512, LAST), shape(rows, 512, f32)] + [shape(rows, 512)] * 9
    scratch = [pltpu.VMEM((128, 2 * rows), f32)] * 2 + [pltpu.VMEM((rows, 512), bf16)] * 3
    return staged(body, "backward", head, values, outs, scratch)


def finish(head, third, other_third, same, slot, dk, dk2, dv, dv2, w_kv, grad, dq, dsk, dsk2, dsv, dsv2, w_self):
    rows = third.shape[0]

    def body(core, get, made, put):
        out, grad_memory, grad_tokens = made
        third, slot = get(0), get(3)
        size = rows // 2
        ahead = jnp.concatenate([mm(third[...], slot[512:, :])[1:, :], mm(get(1)[...], slot[512:, :])[:1, :]], 0)
        out[...] = (mm(third[...], slot[:512, :]) + ahead * get(2)[:, 1:2]).astype(bf16)
        put(0)

        def summed(a, b, here):
            return (get(a)[here, :].astype(f32) + get(b)[here, :].astype(f32)).astype(bf16)

        for block in range(2):
            here = pl.ds(block * size, size)
            grad_memory[here, :] = mm(summed(4, 5, here), get(8)[:, :512], NT) + mm(
                summed(6, 7, here), get(8)[:, 512:], NT
            )
        put(1)
        for block in range(2):
            here = pl.ds(block * size, size)
            w_self = get(15)
            value = get(9)[here, :] + mm(get(10)[here, :], w_self[:, :512], NT)
            value = value + mm(summed(11, 12, here), w_self[:, 512:1024], NT)
            grad_tokens[here, :] = value + mm(summed(13, 14, here), w_self[:, 1024:], NT)
        put(2)

    values = [third, other_third, same, slot, dk, dk2, dv, dv2, w_kv, grad, dq, dsk, dsk2, dsv, dsv2, w_self]
    outs = [shape(rows, 512), shape(rows, 512, f32), shape(rows, 512, f32)]
    return staged(body, "finish", head, values, outs)


def one_hot(rows, columns, target):
    row = lax.broadcasted_iota(jnp.int32, (rows, columns), 0)
    column = lax.broadcasted_iota(jnp.int32, (rows, columns), 1)
    return jnp.where(target(row) == column, 1.0, 0.0).astype(bf16)


def units_apart(value):
    return value.reshape(4, 64, 4, 8).transpose(0, 2, 1, 3).reshape(4, 2048)


def units_together(value):
    return value.reshape(4, 4, 64, 8).transpose(0, 2, 1, 3).reshape(4, 2048)


def spread_rows(row):
    return ((row >> 3) & 1) * 256 + (row >> 4) * 8 + (row & 7)


def norm(resid, gain, bias):
    center = resid - jnp.mean(resid, -1, keepdims=True)
    inverse = lax.rsqrt(jnp.mean(center * center, -1, keepdims=True) + epsilon)
    normed = center * inverse
    return normed * gain + bias, normed, inverse


def norm_back(upstream, normed, inverse, gain):
    scaled = upstream * gain
    mean = jnp.mean(scaled, -1, keepdims=True)
    slope = jnp.mean(scaled * normed, -1, keepdims=True)
    return inverse * (scaled - mean - normed * slope)


def gelu(v):
    root = 0.7978845608028654
    square = v * v
    t = jnp.tanh(root * (v + 0.044715 * square * v))
    up = 0.5 * (1.0 + t)
    return v * up, up + 0.5 * v * (1.0 - t * t) * (root * (1.0 + 3 * 0.044715 * square))


def forward_back_body(
    size, core, get, made, put,
    w_in, w_out, w_cross, hidden_t, inner_grad, second_t, branch_three, branch_two, third_t,
):
    third_out, slot, keep, send, resid_grad, mix_grad, norm_grads = made
    rows = third_out.shape[0]

    def packed(part, side, here, lanes):
        own, other = get(2 * part), get(2 * part + 1)
        return jnp.where(core == side, own[here, lanes], other[here, lanes])

    every = slice(0, 512)
    for side in range(2):
        w_cross[:, 256 * side : 256 * side + 256] = packed(0, side, every, slice(0, 256))

    def first_weights():
        for side in range(2):
            w_in[:, 1024 * side : 1024 * side + 1024] = packed(1, side, every, slice(0, 1024))

    def second_weights():
        for k in range(4):
            for side in range(2):
                w_out[512 * k : 512 * k + 512, 256 * side : 256 * side + 256] = packed(
                    2, side, every, slice(256 * k, 256 + 256 * k)
                )

    order = one_hot(512, 512, spread_rows)

    def slot_weights():
        for side in range(2):
            for level in range(2):
                here = slice(256 * level, 256 * level + 256)
                stack = [packed(3, side, here, slice(256 * k, 256 + 256 * k)) for k in range(2)]
                moved = mm(order, jnp.concatenate(stack, 0)).astype(bf16)
                slot[512 * level : 512 * level + 512, 256 * side : 256 * side + 256] = moved
        put(1)

    mix, first, norms = [get(i) for i in range(8, 11)]
    gain_two, gain_three = norms[1:2, :], norms[2:3, :]
    bias_two, bias_three = norms[4:5, :], norms[5:6, :]
    sums = [jnp.zeros((1, 512), f32) for _ in range(4)]
    for block in range(rows // size):
        here = slice(block * size, block * size + size)
        resid = first[here, :] + mm(mix[here, :], w_cross[...])
        second_block, normed_two, inverse_two = norm(resid, gain_two, bias_two)
        second_low = second_block.astype(bf16)
        second_t[:, here] = second_low.T
        resid = second_block
        slopes = []
        if block == 0:
            first_weights()
            second_weights()
        for k in range(4):
            part = slice(512 * k, 512 * k + 512)
            value, slope = gelu(mm(second_low, w_in[:, part]))
            value = value.astype(bf16)
            hidden_t[part, here] = value.T
            slopes.append(slope)
            resid = resid + mm(value, w_out[part, :])
        third, normed_three, inverse_three = norm(resid, gain_three, bias_three)
        third_low = third.astype(bf16)
        third_out[here, :] = third_low
        third_t[:, here] = mm(third_low, order, NN).astype(bf16).T
        if block == 0:
            slot_weights()
        cot, cot_behind = get(11), get(12)
        grad = mm(cot[here, :], slot[:512, :], NT) + mm(cot_behind[here, :], slot[512:, :], NT)
        sums[1] += jnp.sum(grad * normed_three, 0, keepdims=True)
        sums[3] += jnp.sum(grad, 0, keepdims=True)
        grad = norm_back(grad, normed_three, inverse_three, gain_three)
        branch = grad.astype(bf16)
        branch_three[here, :] = branch
        for k in range(4):
            part = slice(512 * k, 512 * k + 512)
            inner = (mm(branch, w_out[part, :], NT) * slopes[k]).astype(bf16)
            inner_grad[here, part] = inner
            grad = grad + mm(inner, w_in[:, part], NT)
        sums[0] += jnp.sum(grad * normed_two, 0, keepdims=True)
        sums[2] += jnp.sum(grad, 0, keepdims=True)
        grad = norm_back(grad, normed_two, inverse_two, gain_two)
        resid_grad[here, :] = grad
        branch = grad.astype(bf16)
        branch_two[here, :] = branch
        mix_grad[here, :] = mm(branch, w_cross[...], NT).astype(bf16)
    norm_grads[...] = jnp.concatenate(sums + [jnp.zeros((4, 512), f32)], 0)
    for i in (0, 4, 5, 6):
        put(i)

    mix_t = mix[...].T
    for which, target, side in ((3, send, 1 - core), (2, keep, core)):
        columns = pl.ds(pl.multiple_of(side * 256, 256), 256)
        near, behind = cot[:, columns], cot_behind[:, columns]
        for k in range(2):
            lanes = slice(SLOT + 256 * k, SLOT + 256 + 256 * k)
            target[:256, lanes] = mm(third_t[256 * k : 256 * k + 256, :], near).astype(bf16)
            target[256:, lanes] = mm(third_t[256 * k : 256 * k + 256, :], behind).astype(bf16)
        target[:, CROSS : CROSS + 256] = mm(mix_t, branch_two[:, columns]).astype(bf16)
        for k in range(4):
            value = mm(hidden_t[512 * k : 512 * k + 512, :], branch_three[:, columns])
            target[:, OUT + 256 * k : OUT + 256 + 256 * k] = value.astype(bf16)
        start = pl.multiple_of(1024 * side, 1024)
        target[:, :1024] = mm(second_t[...], inner_grad[:, pl.ds(start, 1024)]).astype(bf16)
        put(which)


def forward_back(head, own, other, mix, first, norms, cot, cot_behind, size=384):
    rows = mix.shape[0]
    outs = [shape(rows, 512), shape(1024, 512), shape(512, LATE), shape(512, LATE)]
    outs += [shape(rows, 512, f32), shape(rows, 512), shape(8, 512, f32)]
    scratch = [pltpu.VMEM((512, 2048), bf16), pltpu.VMEM((2048, 512), bf16), pltpu.VMEM((512, 512), bf16)]
    scratch += [pltpu.VMEM((2048, rows), bf16), pltpu.VMEM((rows, 2048), bf16), pltpu.VMEM((512, rows), bf16)]
    scratch += [pltpu.VMEM((rows, 512), bf16)] * 2 + [pltpu.VMEM((512, rows), bf16)]
    body = functools.partial(forward_back_body, size)
    values = [(v, *span) for span in ((CROSS, OUT), (0, CROSS), (OUT, SLOT), (SLOT, LATE)) for v in (own, other)]
    values += [mix, first, norms, cot, cot_behind]
    return staged(body, "forward_back", head, values, outs, scratch, (0, 1, 8, 9, 10, 2, 3, 4, 5, 6, 7, 11, 12))


def combined(keep, arrived):
    return (keep.astype(f32) + arrived.astype(f32)).astype(bf16).reshape(64, 8, keep.shape[1])


def to_owners(mine):
    return lax.all_to_all(mine, "dp", split_axis=0, concat_axis=0, tiled=True)


def owned(sums):
    core = lax.axis_index("head")
    mine = lax.dynamic_slice_in_dim(sums, core * 4, 4, 0)
    other = swap(lax.dynamic_slice_in_dim(sums, 4 - core * 4, 4, 0))
    return mine, other


def joined(mine, other, *slots):
    return jnp.concatenate([by_core(mine[:, s : s + 256], other[:, s : s + 256], 1) for s in slots], 1)


def shards(
    tokens,
    memory,
    segments,
    mem_segments,
    cotangent,
    self_proj,
    self_output,
    cross_query,
    cross_keyval,
    cross_output,
    hidden_in,
    hidden_out,
    slot_proj,
    norm_gain,
    norm_bias,
):
    rows = tokens.shape[0]
    core = lax.axis_index("head")
    head = core.astype(jnp.int32).reshape(1, 1)

    def spread(mine):
        return jnp.broadcast_to(mine[None], (64,) + mine.shape)

    def gathered(block):
        block = lax.all_to_all(block, "dp", split_axis=0, concat_axis=0, tiled=True)
        return block.reshape(512, block.shape[2])

    norms = jnp.pad(jnp.concatenate([norm_gain, norm_bias], 1), ((0, 1), (0, 120)))
    mine, sent = halves(
        self_proj[:, 0], self_proj[:, 1], self_proj[:, 2], self_output, jnp.concatenate([norms, norms], 1),
        cross_query, cross_keyval[:, 0], cross_keyval[:, 1],
    )
    early = spread(by_core(mine, swap(sent), 0))
    early, segments, mem_segments = tie(early, segments, mem_segments)
    early = gathered(early)
    other_tokens, other_memory = swap(tokens), swap(memory)
    qa, self_ka, cross_ka, same = prepare(head, segments, swap(segments), mem_segments, swap(mem_segments))
    qa, hidden_in, hidden_out, slot_proj, cross_output, last_cot = tie(
        qa, hidden_in, hidden_out, slot_proj, cross_output, cotangent
    )
    cot_behind = shift_down(head, cotangent, swap(last_cot[-16:]), same)
    late_mine, late_sent = halves(units_apart(hidden_in), cross_output)
    tall, tall_sent = halves(hidden_out[:8], hidden_out[8:], slot_proj)
    tall_other = swap(tall_sent)
    late = by_core(late_mine, swap(late_sent), 0)
    tall = [by_core(tall[:, :512], tall_other[:, :512], 1), by_core(tall[:, 512:], tall_other[:, 512:], 1)]
    late = spread_early(jnp.concatenate([late] + tall, 1))

    early, late, other_tokens, other_memory, cot_behind, qa, self_ka, cross_ka, same = tie(
        early, late, other_tokens, other_memory, cot_behind, qa, self_ka, cross_ka, same
    )
    early_other = swap(early)
    late = gathered(late)

    query, keyval, w_self, w_out, norms, self_mix, self_lse, first, first_low = forward_self(
        head, early, early_other, tokens, other_tokens, qa, self_ka
    )
    cross_q, mem_keyval, w_query, w_kv, cross_mix, cross_lse = forward_cross(
        head, early, early_other, first_low, memory, other_memory, qa, cross_ka
    )
    late, cross_mix = tie(late, cross_mix)
    third_low, slot, keep, send, grad_resid, grad_cross_mix, norm_grads = forward_back(
        head, late, swap(late), cross_mix, first, norms, cotangent, cot_behind
    )
    other_third = swap(third_low[:16])
    keep, grad_cross_mix = tie(combined(keep, swap(send)), grad_cross_mix)
    late_sums = to_owners(keep)

    keep, send, grad_resid, dk_cross, dk2_cross, dv_cross, dv2_cross, dq, dk, dk2, dv, dv2 = backward(
        head, cross_q, mem_keyval, qa, cross_ka, cross_mix, cross_lse, grad_cross_mix, w_query, grad_resid, norms,
        w_out, tokens, self_mix, query, keyval, qa, self_ka, self_lse, other_tokens, memory, other_memory,
        first_low, norm_grads,
    )
    arrived = swap(send)
    other_keys = [swap(v) for v in (dk2_cross, dv2_cross, dk2, dv2)]
    mine, late_sums, third_low, other_third, *other_keys = tie(
        combined(keep, arrived), late_sums, third_low, other_third, *other_keys
    )
    last_sums = to_owners(mine)

    sums = jnp.sum(late_sums.astype(f32), 0)
    mine, other = owned(sums[:, :OUT])
    tall = [
        jnp.concatenate([half(sums[:, OUT:SLOT], c), half(sums[:, SLOT:], c)], 1) for c in (core, 1 - core)
    ]
    tall, tall_other = tall[0], swap(tall[1])
    out, grad_memory, grad_tokens = finish(
        head, third_low, other_third, same, slot,
        dk_cross, other_keys[0], dv_cross, other_keys[1], w_kv, grad_resid, dq, dk, other_keys[2], dv, other_keys[3], w_self,
    )
    g_hidden_in = units_together(by_core(mine[:, :1024], other[:, :1024], 1))
    g_hidden_out = jnp.concatenate([joined(tall, tall_other, 0), joined(tall, tall_other, 256)])
    g_slot = joined(tall, tall_other, 512)
    out, grad_memory, grad_tokens, last_sums = tie(out, grad_memory, grad_tokens, last_sums)
    last, last_other = owned(jnp.sum(last_sums.astype(f32), 0))
    both = by_core(last[:, :1792].reshape(4, 7, 256), last_other[:, :1792].reshape(4, 7, 256), 2)
    return (
        out,
        grad_tokens,
        grad_memory,
        both[:, :3],
        both[:, 3],
        both[:, 4],
        both[:, 5:],
        joined(mine, other, 1024),
        g_hidden_in,
        g_hidden_out,
        g_slot,
        last[:3, 1792:1796],
        last[:3, 1796:1800],
    )


def solution(mesh):
    split = P(ALL, None)
    cube = P(ALL, None, None)
    flat = P(ALL)
    columns = P(None, ALL)
    in_specs = (split, split, flat, flat, split, cube, split, split, cube, split, split, split, split, columns, columns)
    out_specs = (split, split, split, cube, split, split, cube, split, split, split, split, columns, columns)
    return jax.shard_map(shards, mesh=mesh, in_specs=in_specs, out_specs=out_specs, check_vma=False)
```

```python
import functools

import jax
import jax.numpy as jnp
from jax import lax
from jax.experimental import pallas as pl
from jax.experimental.pallas import tpu as pltpu
from jax.sharding import PartitionSpec as P

HEAD_DIM = 64
epsilon = 1e-05
f32 = jnp.float32
bf16 = jnp.bfloat16
ALL = ("dp", "head")
NT = (((1,), (1,)), ((), ()))
NN = (((1,), (0,)), ((), ()))
TN = (((0,), (0,)), ((), ()))
blocked = -1e30


def mm(a, b, dims=NN):
    return lax.dot_general(a, b, dims, preferred_element_type=f32)


def low_half(shape):
    return lax.broadcasted_iota(jnp.int32, shape, 1) < HEAD_DIM


def pieces(x):
    hi = x.astype(bf16)
    rest = x - hi.astype(f32)
    mid = rest.astype(bf16)
    return hi, mid, (rest - mid.astype(f32)).astype(bf16)


def attention(q_ref, kv_ref, qa_ref, ka_ref, o_ref, lse_ref, size=768):
    rows, width = q_ref.shape
    total = kv_ref.shape[0]

    def pair(p):
        here = slice(128 * p, 128 * p + 128)
        key_low = low_half((total, 128))
        keys, key_extra = kv_ref[:, here], ka_ref[...]
        key_tiles = [jnp.where(key_low, keys, key_extra), jnp.where(key_low, key_extra, keys)]
        turned = kv_ref[:, slice(128 * p + width, 128 * p + width + 128)].T
        ones = jnp.ones((16, total), bf16)
        value_tiles = [jnp.concatenate([turned[64 * h : 64 * h + 64], ones], 0) for h in range(2)]
        low = low_half((size, 128))
        for block in range(rows // size):
            span = slice(block * size, block * size + size)
            q = q_ref[span, here] * bf16(HEAD_DIM**-0.5)
            qa = qa_ref[span, :]
            outs, sums = [], []
            for h in range(2):
                q_tile = jnp.where(low, q, qa) if h == 0 else jnp.where(low, qa, q)
                scores = mm(key_tiles[h], q_tile, NT)
                peak = jnp.max(scores, 0, keepdims=True)
                mixed = mm(value_tiles[h], jnp.exp(scores - peak).astype(bf16))
                count = mixed[64:65, :]
                outs.append(mixed[:64, :] * (1.0 / count))
                sums.append(peak + jnp.log(count))
            o_ref[span, here] = jnp.concatenate(outs, 0).T.astype(bf16)
            lse_ref[p, :, span] = jnp.concatenate(sums + [jnp.zeros((6, size), f32)], 0)

    for p in range(width // 128):
        pair(p)


def attention_back(
    sources, qa_ref, ka_ref, lse_ref, dq_ref, dk_ref, dk2_ref, dv_ref, dv2_ref, dkt, dvt, size=384
):
    rows, width = dq_ref.shape
    total = ka_ref.shape[0]

    for p in range(width // 128):
        lanes = slice(128 * p, 128 * p + 128)
        q_ref, k_ref, v_ref, o_ref, do_ref = sources(p)
        key_low = low_half((total, 128))
        keys, key_extra = k_ref[...], ka_ref[...]
        values = v_ref[...]
        ones = jnp.ones_like(values)
        key_tiles = [jnp.where(key_low, keys, key_extra), jnp.where(key_low, key_extra, keys)]
        value_tiles = [jnp.where(key_low, values, ones), jnp.where(key_low, ones, values)]
        low = low_half((size, 128))
        lane = lax.broadcasted_iota(jnp.int32, (size, 128), 1)
        lse_columns = lse_ref[p].T
        for block in range(rows // size):
            here = slice(block * size, block * size + size)
            q = q_ref[here, :] * bf16(HEAD_DIM**-0.5)
            qa = qa_ref[here, :]
            do = do_ref[here, :]
            product = do.astype(f32) * o_ref[here, :].astype(f32)
            lse = lse_columns[here, :]
            q_turned, do_turned = q.T, do.T
            dqs = []
            for h in range(2):
                spare = HEAD_DIM * (1 - h)
                mine = low if h == 0 else jnp.logical_not(low)
                delta = jnp.sum(jnp.where(mine, product, 0.0), -1, keepdims=True)
                d0, d1, d2 = pieces(-delta)
                l0, l1, l2 = pieces(-lse[:, h : h + 1])
                q_extra = jnp.where(
                    lane == spare + 3, l0, jnp.where(lane == spare + 4, l1, jnp.where(lane == spare + 5, l2, qa))
                )
                do_extra = jnp.where(
                    lane == spare, d0, jnp.where(lane == spare + 1, d1, jnp.where(lane == spare + 2, d2, bf16(0)))
                )
                probs = jnp.exp(mm(jnp.where(mine, q, q_extra), key_tiles[h], NT))
                grad = mm(jnp.where(mine, do, do_extra), value_tiles[h], NT)
                low_probs = probs.astype(bf16)
                ds = (probs * grad).astype(bf16)
                dqs.append(mm(ds, keys))
                part = slice(HEAD_DIM * h, HEAD_DIM * h + HEAD_DIM)
                new_dk = mm(q_turned[part, :], ds)
                new_dv = mm(do_turned[part, :], low_probs)
                if block == 0:
                    dkt[part, :] = new_dk
                    dvt[part, :] = new_dv
                else:
                    dkt[part, :] += new_dk
                    dvt[part, :] += new_dv
            dq_ref[here, lanes] = (jnp.where(low, dqs[0], dqs[1]) * HEAD_DIM**-0.5).astype(bf16)
        for turned, near, far in ((dkt, dk_ref, dk2_ref), (dvt, dv_ref, dv2_ref)):
            near[:, lanes] = turned[:, :rows].astype(bf16).T
            far[:, lanes] = turned[:, rows:].astype(bf16).T


def swap(value):
    return lax.ppermute(value, "head", [(0, 1), (1, 0)])


def tie(*values):
    return lax.optimization_barrier(values)


def by_core(own, other, axis):
    first = lax.axis_index("head") == 0
    return jnp.where(first, jnp.concatenate([own, other], axis), jnp.concatenate([other, own], axis))


def half(value, core):
    width = value.shape[-1] // 2
    return lax.dynamic_slice_in_dim(value, core * width, width, value.ndim - 1)


def halves(*weights):
    sides = [jnp.concatenate([w[:, w.shape[1] // 2 * i : w.shape[1] // 2 * (i + 1)] for w in weights], 1) for i in (0, 1)]
    first = lax.axis_index("head") == 0
    return jnp.where(first, sides[0], sides[1]), jnp.where(first, sides[1], sides[0])


EARLY = 1152
MIDDLE = 768
LATE = 2816
CROSS, OUT, SLOT = 1024, 1280, 2304


def staged(body, name, head, values, outs, scratch=(), order=None, limit=60):
    count, results = len(values), len(outs)
    spans = [v[1:] if isinstance(v, tuple) else None for v in values]
    values = [v[0] if isinstance(v, tuple) else v for v in values]
    sizes = [v.shape if span is None else (v.shape[0], span[1] - span[0]) for v, span in zip(values, spans)]

    def kernel(*refs):
        head_ref, sources, targets = refs[0], refs[1 : 1 + count], refs[1 + count : 1 + count + results]
        rest = refs[1 + count + results :]
        inside, made = rest[:count], rest[count : count + results]
        in_sems, out_sems = rest[count + results], rest[count + results + 1]
        loads = []
        for i in range(count):
            source = sources[i] if spans[i] is None else sources[i].at[:, spans[i][0] : spans[i][1]]
            loads.append(pltpu.make_async_copy(source, inside[i], in_sems.at[i]))
        for i in order or range(count):
            loads[i].start()
        waited, stores = set(), []

        def get(i):
            if i not in waited:
                loads[i].wait()
                waited.add(i)
            return inside[i]

        def put(i):
            store = pltpu.make_async_copy(made[i], targets[i], out_sems.at[i])
            store.start()
            stores.append(store)

        body(head_ref[0, 0], get, made, put, *rest[count + results + 2 :])
        for i in range(count):
            get(i)
        for store in stores:
            store.wait()

    return pl.pallas_call(
        kernel,
        in_specs=[pl.BlockSpec(memory_space=pltpu.SMEM)] + [pl.BlockSpec(memory_space=pltpu.HBM)] * count,
        out_specs=[pl.BlockSpec(memory_space=pltpu.HBM)] * results,
        out_shape=outs,
        scratch_shapes=[pltpu.VMEM(size, v.dtype) for size, v in zip(sizes, values)]
        + [pltpu.VMEM(o.shape, o.dtype) for o in outs]
        + [pltpu.SemaphoreType.DMA((count,)), pltpu.SemaphoreType.DMA((results,))]
        + list(scratch),
        compiler_params=pltpu.CompilerParams(vmem_limit_bytes=limit * 2**20),
        name=name,
    )(head, *values)


def in_fours(rows):
    place = lax.broadcasted_iota(jnp.int32, (1, 512), 1) & 3
    moved = {s: pltpu.roll(rows, s % 512, 1) for s in range(-3, 4)}
    made = []
    for base in (0, 4):
        for c in range(4):
            row = jnp.zeros((1, 512), f32)
            for n in range(4):
                row = row + jnp.where(place == n, moved[n - c][base + n : base + n + 1, :], 0.0)
            made.append(row)
    return jnp.concatenate(made, 0)


def shape(rows, columns, kind=bf16):
    return jax.ShapeDtypeStruct((rows, columns), kind)


def prepare(head, own, other, mem, mem2):
    rows = own.shape[0]

    def body(core, get, made, put):
        qa, ka, cross_ka, same = made
        segs = [get(i)[...].astype(f32).reshape(1, rows) for i in range(4)]
        segs = jnp.concatenate(segs + [jnp.zeros((4, rows), f32)], 0)
        lane = lax.broadcasted_iota(jnp.int32, (rows, 128), 1) & 63
        marks, ones = lane < 3, (lane >= 3) & (lane < 6)
        number = lane.astype(f32)
        columns = segs.T
        qa[...] = jnp.where(marks & (columns[:, 0:1] != number), blocked, 0.0).astype(bf16)
        for target, first in ((ka, 0), (cross_ka, 2)):
            for i in range(2):
                match = (marks & (columns[:, first + i : first + i + 1] == number)) | ones
                target[rows * i : rows * i + rows, :] = jnp.where(match, 1.0, 0.0).astype(bf16)
        place = lax.broadcasted_iota(jnp.int32, (1, rows), 1)
        down, up = pltpu.roll(segs, 1, 1), pltpu.roll(segs, rows - 1, 1)
        last = jnp.where(core == 1, down[1:2, :], -1.0)
        next_one = jnp.where(core == 0, up[1:2, :], -1.0)
        same_down = jnp.where(jnp.where(place == 0, last, down[0:1, :]) == segs[0:1, :], 1.0, 0.0)
        same_up = jnp.where(jnp.where(place == rows - 1, next_one, up[0:1, :]) == segs[0:1, :], 1.0, 0.0)
        columns = jnp.concatenate([same_down, same_up, jnp.zeros((6, rows), f32)], 0).T
        lane = lax.broadcasted_iota(jnp.int32, (rows, 128), 1)
        same[...] = jnp.where(lane == 0, columns[:, 0:1], columns[:, 1:2])
        for i in range(4):
            put(i)

    outs = [shape(rows, 128), shape(2 * rows, 128), shape(2 * rows, 128), shape(rows, 128, f32)]
    return staged(body, "prepare", head, [own, other, mem, mem2], outs)


def shift_down(head, cot, far, same):
    rows = cot.shape[0]

    def body(core, get, made, put):
        (behind,) = made
        moved = pltpu.roll(get(0)[...].astype(f32), 1, 0)
        row = lax.broadcasted_iota(jnp.int32, (rows, 512), 0)
        moved = jnp.where(row == 0, get(1)[...].astype(f32)[15:16, :], moved)
        behind[...] = jnp.where(get(2)[:, 0:1] > 0.0, moved, 0.0).astype(bf16)
        put(0)

    return staged(body, "shift_down", head, [cot, far, same], [shape(rows, 512)])[0]


def spread_kernel(block, out):
    out[...] = jnp.broadcast_to(block[...][None], out.shape)


def spread_early(block):
    return pl.pallas_call(
        spread_kernel,
        grid=(8,),
        in_specs=[pl.BlockSpec(block.shape, lambda i: (0, 0))],
        out_specs=pl.BlockSpec((8,) + block.shape, lambda i: (i, 0, 0)),
        out_shape=jax.ShapeDtypeStruct((64,) + block.shape, bf16),
        name="spread_early",
    )(block)


def both_halves(core, own, other, slot):
    here = slice(256 * slot, 256 * slot + 256)
    a, b = own[:, here], other[:, here]
    return jnp.concatenate([jnp.where(core == 0, a, b), jnp.where(core == 0, b, a)], 1)


def both_parts(own, other, *edges):
    return [(v, a, b) for a, b in zip(edges, edges[1:]) for v in (own, other)]


def forward_self(head, own, other, tok, tok2, qa, ka):
    rows = tok.shape[0]
    values = both_parts(own, other, 0, 256, 768, EARLY) + [tok, tok2, qa, ka]

    def body(core, get, made, put):
        q, kv, w_self, w_out, norms, mix, lse, first, low = made
        w_self[:, :512] = both_halves(core, get(0), get(1), 0)
        tok = get(6)
        q[...] = mm(tok[...], w_self[:, :512]).astype(bf16)
        put(0)
        for part in range(2):
            w_self[:, 512 * part + 512 : 512 * part + 1024] = both_halves(core, get(2), get(3), part)
        put(2)
        kv[:rows, :] = mm(tok[...], w_self[:, 512:]).astype(bf16)
        kv[rows:, :] = mm(get(7)[...], w_self[:, 512:]).astype(bf16)
        put(1)
        w_out[...] = both_halves(core, get(4), get(5), 0)
        put(3)
        turned = in_fours(get(4)[:, 256:].astype(f32).T[:8, :])
        norms[...] = jnp.concatenate([turned[:3, :], turned[4:7, :], jnp.zeros((2, 512), f32)], 0)
        put(4)
        attention(q, kv, get(8), get(9), mix, lse)
        put(5)
        put(6)
        size = rows // 2
        for block in range(2):
            here = slice(block * size, block * size + size)
            value = tok[here, :].astype(f32) + mm(mix[here, :], w_out[...])
            value = norm(value, norms[0:1, :], norms[3:4, :])[0]
            first[here, :] = value
            low[here, :] = value.astype(bf16)
        put(8)
        put(7)

    outs = [shape(rows, 512), shape(2 * rows, 1024), shape(512, 1536), shape(512, 512), shape(8, 512, f32)]
    outs += [shape(rows, 512), jax.ShapeDtypeStruct((4, 8, rows), f32), shape(rows, 512, f32), shape(rows, 512)]
    return staged(body, "forward_self", head, values, outs, order=(0, 1, 6, 2, 3, 7, 8, 9, 4, 5))


def forward_cross(head, own, other, low, mem, mem2, qa, ka):
    rows = mem.shape[0]
    values = both_parts(own, other, EARLY, EARLY + 256, EARLY + MIDDLE) + [low, mem, mem2, qa, ka]

    def body(core, get, made, put):
        q, kv, w_query, w_kv, mix, lse = made
        w_query[...] = both_halves(core, get(0), get(1), 0)
        put(2)
        q[...] = mm(get(4)[...], w_query[...]).astype(bf16)
        put(0)
        for part in range(2):
            w_kv[:, 512 * part : 512 * part + 512] = both_halves(core, get(2), get(3), part)
        put(3)
        kv[:rows, :] = mm(get(5)[...], w_kv[...]).astype(bf16)
        kv[rows:, :] = mm(get(6)[...], w_kv[...]).astype(bf16)
        put(1)
        attention(q, kv, get(7), get(8), mix, lse)
        put(4)
        put(5)

    outs = [shape(rows, 512), shape(2 * rows, 1024), shape(512, 512), shape(512, 1024)]
    outs += [shape(rows, 512), jax.ShapeDtypeStruct((4, 8, rows), f32)]
    return staged(body, "forward_cross", head, values, outs, order=(0, 1, 4, 2, 3, 5, 6, 7, 8))


LAST = 1920


def backward(
    head, cross_q, mem_kv, qa, cross_ka, cross_mix, cross_lse, cross_grad, w_query, resid_grad, norms, w_out,
    tok, mix, q, kv, ka, lse, tok2, mem, mem2, low, norm_grads,
):
    rows = tok.shape[0]
    values = []
    for p in range(4):
        columns = (128 * p, 128 * p + 128)
        values += [(cross_q, *columns), (mem_kv, *columns), (mem_kv, 512 + columns[0], 512 + columns[1])]
        values += [(cross_mix, *columns), (cross_grad, *columns)]
    values += [qa, cross_ka, cross_lse, w_query, resid_grad, norms, w_out, tok, mix, q, kv, ka, lse]
    values += [tok2, mem, mem2, low, norm_grads]
    order = [20, 21, 22] + list(range(20)) + list(range(23, len(values)))

    def body(core, get, made, put, dkt, dvt, dq_cross, branch, mix_grad):
        keep, send, resid_out, dk_c, dk2_c, dv_c, dv2_c, dq, dk, dk2, dv, dv2 = made
        qa = get(20)
        attention_back(
            lambda p: [get(5 * p + i) for i in range(5)], qa, get(21), get(22), dq_cross, dk_c, dk2_c, dv_c, dv2_c, dkt, dvt
        )
        for i in (4, 6, 3, 5):
            put(i)
        w_query, resid_grad, norms, w_out, tok, mix = [get(i) for i in range(23, 29)]
        size = rows // 2
        sums = [jnp.zeros((1, 512), f32) for _ in range(2)]
        for block in range(2):
            here = slice(block * size, block * size + size)
            resid = tok[here, :].astype(f32) + mm(mix[here, :], w_out[...])
            _, normed, inverse = norm(resid, norms[0:1, :], norms[3:4, :])
            grad = resid_grad[here, :] + mm(dq_cross[here, :], w_query[...], NT)
            sums[0] += jnp.sum(grad * normed, 0, keepdims=True)
            sums[1] += jnp.sum(grad, 0, keepdims=True)
            grad = norm_back(grad, normed, inverse, norms[0:1, :])
            resid_out[here, :] = grad
            branch[here, :] = grad.astype(bf16)
            mix_grad[here, :] = mm(branch[here, :], w_out[...], NT).astype(bf16)
        put(2)
        q, kv = get(29), get(30)

        def sources(p):
            here, there = slice(128 * p, 128 * p + 128), slice(512 + 128 * p, 640 + 128 * p)
            return q.at[:, here], kv.at[:, here], kv.at[:, there], mix.at[:, here], mix_grad.at[:, here]

        attention_back(sources, qa, get(31), get(32), dq, dk, dk2, dv, dv2, dkt, dvt)
        for i in (9, 11, 7, 8, 10):
            put(i)

        tok2, mem, mem2, low, norm_grads = [get(i) for i in range(33, 38)]
        sides = (core, 1 - core)
        columns = [pl.ds(pl.multiple_of(side * 256, 256), 256) for side in sides]

        jobs = []

        def store(slot, *pairs):
            jobs.append((slot, pairs))

        blank = jnp.zeros((1, 512), f32)
        every = jnp.concatenate([sums[0], norm_grads[0:2, :], blank, sums[1], norm_grads[2:4, :], blank], 0)
        padded = jnp.concatenate([in_fours(every), jnp.zeros((120, 512), f32)], 0).T.astype(bf16)
        for target in (keep, send):
            target[:, 1792:] = padded
        store(4, (low[...].T, dq_cross))
        store(3, (mix[...].T, branch))
        near, far = mem[...].T, mem2[...].T
        store(5, (near, dk_c), (far, dk2_c))
        store(6, (near, dv_c), (far, dv2_c))
        near, far = tok[...].T, tok2[...].T
        store(0, (near, dq))
        store(1, (near, dk), (far, dk2))
        store(2, (near, dv), (far, dv2))
        for which, target, here in ((1, send, columns[1]), (0, keep, columns[0])):
            for slot, pairs in jobs:
                value = sum(mm(left, right[:, here]) for left, right in pairs)
                target[:, 256 * slot : 256 * slot + 256] = value.astype(bf16)
            put(which)

    outs = [shape(512, LAST), shape(512, LAST), shape(rows, 512, f32)] + [shape(rows, 512)] * 9
    scratch = [pltpu.VMEM((128, 2 * rows), f32)] * 2 + [pltpu.VMEM((rows, 512), bf16)] * 3
    return staged(body, "backward", head, values, outs, scratch, order)


def finish(head, third, other_third, same, slot, dk, dk2, dv, dv2, w_kv, grad, dq, dsk, dsk2, dsv, dsv2, w_self):
    rows = third.shape[0]

    def body(core, get, made, put):
        out, grad_memory, grad_tokens = made
        third, slot = get(0), get(3)
        size = rows // 2
        ahead = jnp.concatenate([mm(third[...], slot[512:, :])[1:, :], mm(get(1)[...], slot[512:, :])[:1, :]], 0)
        out[...] = (mm(third[...], slot[:512, :]) + ahead * get(2)[:, 1:2]).astype(bf16)
        put(0)

        def summed(a, b, here):
            return (get(a)[here, :].astype(f32) + get(b)[here, :].astype(f32)).astype(bf16)

        for block in range(2):
            here = pl.ds(block * size, size)
            grad_memory[here, :] = mm(summed(4, 5, here), get(8)[:, :512], NT) + mm(
                summed(6, 7, here), get(8)[:, 512:], NT
            )
        put(1)
        for block in range(2):
            here = pl.ds(block * size, size)
            w_self = get(15)
            value = get(9)[here, :] + mm(get(10)[here, :], w_self[:, :512], NT)
            value = value + mm(summed(11, 12, here), w_self[:, 512:1024], NT)
            grad_tokens[here, :] = value + mm(summed(13, 14, here), w_self[:, 1024:], NT)
        put(2)

    values = [third, other_third, same, slot, dk, dk2, dv, dv2, w_kv, grad, dq, dsk, dsk2, dsv, dsv2, w_self]
    outs = [shape(rows, 512), shape(rows, 512, f32), shape(rows, 512, f32)]
    return staged(body, "finish", head, values, outs)


def one_hot(rows, columns, target):
    row = lax.broadcasted_iota(jnp.int32, (rows, columns), 0)
    column = lax.broadcasted_iota(jnp.int32, (rows, columns), 1)
    return jnp.where(target(row) == column, 1.0, 0.0).astype(bf16)


def units_apart(value):
    return value.reshape(4, 64, 4, 8).transpose(0, 2, 1, 3).reshape(4, 2048)


def units_together(value):
    return value.reshape(4, 4, 64, 8).transpose(0, 2, 1, 3).reshape(4, 2048)


def spread_rows(row):
    return ((row >> 3) & 1) * 256 + (row >> 4) * 8 + (row & 7)


def norm(resid, gain, bias):
    center = resid - jnp.mean(resid, -1, keepdims=True)
    inverse = lax.rsqrt(jnp.mean(center * center, -1, keepdims=True) + epsilon)
    normed = center * inverse
    return normed * gain + bias, normed, inverse


def norm_back(upstream, normed, inverse, gain):
    scaled = upstream * gain
    mean = jnp.mean(scaled, -1, keepdims=True)
    slope = jnp.mean(scaled * normed, -1, keepdims=True)
    return inverse * (scaled - mean - normed * slope)


def gelu(v):
    root = 0.7978845608028654
    square = v * v
    t = jnp.tanh(root * (v + 0.044715 * square * v))
    up = 0.5 * (1.0 + t)
    return v * up, up + 0.5 * v * (1.0 - t * t) * (root * (1.0 + 3 * 0.044715 * square))


def forward_back_body(
    size, core, get, made, put,
    w_in, w_out, w_cross, hidden_t, inner_grad, second_t, branch_three, branch_two, third_t,
):
    third_out, slot, keep, send, resid_grad, mix_grad, norm_grads = made
    rows = third_out.shape[0]

    def packed(part, side, here, lanes):
        own, other = get(2 * part), get(2 * part + 1)
        return jnp.where(core == side, own[here, lanes], other[here, lanes])

    every = slice(0, 512)
    for side in range(2):
        w_cross[:, 256 * side : 256 * side + 256] = packed(0, side, every, slice(0, 256))

    def first_weights():
        for side in range(2):
            w_in[:, 1024 * side : 1024 * side + 1024] = packed(1, side, every, slice(0, 1024))

    def second_weights():
        for k in range(4):
            for side in range(2):
                w_out[512 * k : 512 * k + 512, 256 * side : 256 * side + 256] = packed(
                    2, side, every, slice(256 * k, 256 + 256 * k)
                )

    order = one_hot(512, 512, spread_rows)

    def slot_weights():
        for side in range(2):
            for level in range(2):
                here = slice(256 * level, 256 * level + 256)
                stack = [packed(3, side, here, slice(256 * k, 256 + 256 * k)) for k in range(2)]
                moved = mm(order, jnp.concatenate(stack, 0)).astype(bf16)
                slot[512 * level : 512 * level + 512, 256 * side : 256 * side + 256] = moved
        put(1)

    mix, first, norms = [get(i) for i in range(8, 11)]
    gain_two, gain_three = norms[1:2, :], norms[2:3, :]
    bias_two, bias_three = norms[4:5, :], norms[5:6, :]
    sums = [jnp.zeros((1, 512), f32) for _ in range(4)]
    for block in range(rows // size):
        here = slice(block * size, block * size + size)
        resid = first[here, :] + mm(mix[here, :], w_cross[...])
        second_block, normed_two, inverse_two = norm(resid, gain_two, bias_two)
        second_low = second_block.astype(bf16)
        second_t[:, here] = second_low.T
        resid = second_block
        slopes = []
        if block == 0:
            first_weights()
            second_weights()
        for k in range(4):
            part = slice(512 * k, 512 * k + 512)
            value, slope = gelu(mm(second_low, w_in[:, part]))
            value = value.astype(bf16)
            hidden_t[part, here] = value.T
            slopes.append(slope)
            resid = resid + mm(value, w_out[part, :])
        third, normed_three, inverse_three = norm(resid, gain_three, bias_three)
        third_low = third.astype(bf16)
        third_out[here, :] = third_low
        third_t[:, here] = mm(third_low, order, NN).astype(bf16).T
        if block == 0:
            slot_weights()
        cot, cot_behind = get(11), get(12)
        grad = mm(cot[here, :], slot[:512, :], NT) + mm(cot_behind[here, :], slot[512:, :], NT)
        sums[1] += jnp.sum(grad * normed_three, 0, keepdims=True)
        sums[3] += jnp.sum(grad, 0, keepdims=True)
        grad = norm_back(grad, normed_three, inverse_three, gain_three)
        branch = grad.astype(bf16)
        branch_three[here, :] = branch
        for k in range(4):
            part = slice(512 * k, 512 * k + 512)
            inner = (mm(branch, w_out[part, :], NT) * slopes[k]).astype(bf16)
            inner_grad[here, part] = inner
            grad = grad + mm(inner, w_in[:, part], NT)
        sums[0] += jnp.sum(grad * normed_two, 0, keepdims=True)
        sums[2] += jnp.sum(grad, 0, keepdims=True)
        grad = norm_back(grad, normed_two, inverse_two, gain_two)
        resid_grad[here, :] = grad
        branch = grad.astype(bf16)
        branch_two[here, :] = branch
        mix_grad[here, :] = mm(branch, w_cross[...], NT).astype(bf16)
    norm_grads[...] = jnp.concatenate(sums + [jnp.zeros((4, 512), f32)], 0)
    for i in (0, 4, 5, 6):
        put(i)

    mix_t = mix[...].T
    for which, target, side in ((3, send, 1 - core), (2, keep, core)):
        columns = pl.ds(pl.multiple_of(side * 256, 256), 256)
        near, behind = cot[:, columns], cot_behind[:, columns]
        for k in range(2):
            lanes = slice(SLOT + 256 * k, SLOT + 256 + 256 * k)
            target[:256, lanes] = mm(third_t[256 * k : 256 * k + 256, :], near).astype(bf16)
            target[256:, lanes] = mm(third_t[256 * k : 256 * k + 256, :], behind).astype(bf16)
        target[:, CROSS : CROSS + 256] = mm(mix_t, branch_two[:, columns]).astype(bf16)
        for k in range(4):
            value = mm(hidden_t[512 * k : 512 * k + 512, :], branch_three[:, columns])
            target[:, OUT + 256 * k : OUT + 256 + 256 * k] = value.astype(bf16)
        start = pl.multiple_of(1024 * side, 1024)
        target[:, :1024] = mm(second_t[...], inner_grad[:, pl.ds(start, 1024)]).astype(bf16)
        put(which)


def forward_back(head, own, other, mix, first, norms, cot, cot_behind, size=384):
    rows = mix.shape[0]
    outs = [shape(rows, 512), shape(1024, 512), shape(512, LATE), shape(512, LATE)]
    outs += [shape(rows, 512, f32), shape(rows, 512), shape(8, 512, f32)]
    scratch = [pltpu.VMEM((512, 2048), bf16), pltpu.VMEM((2048, 512), bf16), pltpu.VMEM((512, 512), bf16)]
    scratch += [pltpu.VMEM((2048, rows), bf16), pltpu.VMEM((rows, 2048), bf16), pltpu.VMEM((512, rows), bf16)]
    scratch += [pltpu.VMEM((rows, 512), bf16)] * 2 + [pltpu.VMEM((512, rows), bf16)]
    body = functools.partial(forward_back_body, size)
    values = [(v, *span) for span in ((CROSS, OUT), (0, CROSS), (OUT, SLOT), (SLOT, LATE)) for v in (own, other)]
    values += [mix, first, norms, cot, cot_behind]
    return staged(body, "forward_back", head, values, outs, scratch, (0, 1, 8, 9, 10, 2, 3, 4, 5, 6, 7, 11, 12))


def combined(keep, arrived):
    return (keep.astype(f32) + arrived.astype(f32)).astype(bf16).reshape(64, 8, keep.shape[1])


def to_owners(mine):
    return lax.all_to_all(mine, "dp", split_axis=0, concat_axis=0, tiled=True)


def owned(sums):
    core = lax.axis_index("head")
    mine = lax.dynamic_slice_in_dim(sums, core * 4, 4, 0)
    other = swap(lax.dynamic_slice_in_dim(sums, 4 - core * 4, 4, 0))
    return mine, other


def joined(mine, other, *slots):
    return jnp.concatenate([by_core(mine[:, s : s + 256], other[:, s : s + 256], 1) for s in slots], 1)


def shards(
    tokens,
    memory,
    segments,
    mem_segments,
    cotangent,
    self_proj,
    self_output,
    cross_query,
    cross_keyval,
    cross_output,
    hidden_in,
    hidden_out,
    slot_proj,
    norm_gain,
    norm_bias,
):
    rows = tokens.shape[0]
    core = lax.axis_index("head")
    head = core.astype(jnp.int32).reshape(1, 1)

    def spread(mine):
        return jnp.broadcast_to(mine[None], (64,) + mine.shape)

    def gathered(block):
        block = lax.all_to_all(block, "dp", split_axis=0, concat_axis=0, tiled=True)
        return block.reshape(512, block.shape[2])

    norms = jnp.pad(jnp.concatenate([norm_gain, norm_bias], 1), ((0, 1), (0, 120)))
    mine, sent = halves(
        self_proj[:, 0], self_proj[:, 1], self_proj[:, 2], self_output, jnp.concatenate([norms, norms], 1),
        cross_query, cross_keyval[:, 0], cross_keyval[:, 1],
    )
    early = spread(by_core(mine, swap(sent), 0))
    early, segments, mem_segments = tie(early, segments, mem_segments)
    early = gathered(early)
    other_tokens, other_memory = swap(tokens), swap(memory)
    qa, self_ka, cross_ka, same = prepare(head, segments, swap(segments), mem_segments, swap(mem_segments))
    qa, hidden_in, hidden_out, slot_proj, cross_output, last_cot = tie(
        qa, hidden_in, hidden_out, slot_proj, cross_output, cotangent
    )
    cot_behind = shift_down(head, cotangent, swap(last_cot[-16:]), same)
    late_mine, late_sent = halves(units_apart(hidden_in), cross_output)
    tall, tall_sent = halves(hidden_out[:8], hidden_out[8:], slot_proj)
    tall_other = swap(tall_sent)
    late = by_core(late_mine, swap(late_sent), 0)
    tall = [by_core(tall[:, :512], tall_other[:, :512], 1), by_core(tall[:, 512:], tall_other[:, 512:], 1)]
    late = spread_early(jnp.concatenate([late] + tall, 1))

    early, late, other_tokens, other_memory, cot_behind, qa, self_ka, cross_ka, same = tie(
        early, late, other_tokens, other_memory, cot_behind, qa, self_ka, cross_ka, same
    )
    early_other = swap(early)
    late = gathered(late)

    query, keyval, w_self, w_out, norms, self_mix, self_lse, first, first_low = forward_self(
        head, early, early_other, tokens, other_tokens, qa, self_ka
    )
    cross_q, mem_keyval, w_query, w_kv, cross_mix, cross_lse = forward_cross(
        head, early, early_other, first_low, memory, other_memory, qa, cross_ka
    )
    late, cross_mix = tie(late, cross_mix)
    third_low, slot, keep, send, grad_resid, grad_cross_mix, norm_grads = forward_back(
        head, late, swap(late), cross_mix, first, norms, cotangent, cot_behind
    )
    other_third = swap(third_low[:16])
    keep, grad_cross_mix = tie(combined(keep, swap(send)), grad_cross_mix)
    late_sums = to_owners(keep)

    keep, send, grad_resid, dk_cross, dk2_cross, dv_cross, dv2_cross, dq, dk, dk2, dv, dv2 = backward(
        head, cross_q, mem_keyval, qa, cross_ka, cross_mix, cross_lse, grad_cross_mix, w_query, grad_resid, norms,
        w_out, tokens, self_mix, query, keyval, self_ka, self_lse, other_tokens, memory, other_memory,
        first_low, norm_grads,
    )
    arrived = swap(send)
    other_keys = [swap(v) for v in (dk2_cross, dv2_cross, dk2, dv2)]
    mine, late_sums, third_low, other_third, *other_keys = tie(
        combined(keep, arrived), late_sums, third_low, other_third, *other_keys
    )
    last_sums = to_owners(mine)

    sums = jnp.sum(late_sums.astype(f32), 0)
    mine, other = owned(sums[:, :OUT])
    tall = [
        jnp.concatenate([half(sums[:, OUT:SLOT], c), half(sums[:, SLOT:], c)], 1) for c in (core, 1 - core)
    ]
    tall, tall_other = tall[0], swap(tall[1])
    out, grad_memory, grad_tokens = finish(
        head, third_low, other_third, same, slot,
        dk_cross, other_keys[0], dv_cross, other_keys[1], w_kv, grad_resid, dq, dk, other_keys[2], dv, other_keys[3], w_self,
    )
    g_hidden_in = units_together(by_core(mine[:, :1024], other[:, :1024], 1))
    g_hidden_out = jnp.concatenate([joined(tall, tall_other, 0), joined(tall, tall_other, 256)])
    g_slot = joined(tall, tall_other, 512)
    out, grad_memory, grad_tokens, last_sums = tie(out, grad_memory, grad_tokens, last_sums)
    last, last_other = owned(jnp.sum(last_sums.astype(f32), 0))
    both = by_core(last[:, :1792].reshape(4, 7, 256), last_other[:, :1792].reshape(4, 7, 256), 2)
    return (
        out,
        grad_tokens,
        grad_memory,
        both[:, :3],
        both[:, 3],
        both[:, 4],
        both[:, 5:],
        joined(mine, other, 1024),
        g_hidden_in,
        g_hidden_out,
        g_slot,
        last[:3, 1792:1796],
        last[:3, 1796:1800],
    )


def solution(mesh):
    split = P(ALL, None)
    cube = P(ALL, None, None)
    flat = P(ALL)
    columns = P(None, ALL)
    in_specs = (split, split, flat, flat, split, cube, split, split, cube, split, split, split, split, columns, columns)
    out_specs = (split, split, split, cube, split, split, cube, split, split, split, split, columns, columns)
    return jax.shard_map(shards, mesh=mesh, in_specs=in_specs, out_specs=out_specs, check_vma=False)
```
